256 devices in a mesh: island: 8 (over z_hi, core), fsdp: 32 (over z_lo, y, x).
Axes of the slice: x: 4, y: 4, z: 8 (z_hi: 4, z_lo: 2; z = z_hi * 2 + z_lo), core: 2. Of those that a mesh axis runs over, the one named last changes fastest.
Arguments:
- base_in: float32 [2, 2048, 2048], P(None, 'fsdp')
- base_out: float32 [2, 1024, 2048], P(None, 'fsdp')
- local_in: bfloat16 [8, 2, 2048, 2048], P('island', None, 'fsdp')
- local_out: bfloat16 [8, 2, 1024, 2048], P('island', None, 'fsdp')
- mom_in: float32 [2, 2048, 2048], P(None, 'fsdp'), may hold values from -0.12 to 0.12
- mom_out: float32 [2, 1024, 2048], P(None, 'fsdp'), may hold values from -0.12 to 0.12
- exp_in: int32 [2, 2048], P(None, 'fsdp'), may hold values from -12 to -8
- exp_out: int32 [2, 1024], P(None, 'fsdp'), may hold values from -12 to -8
- tokens: bfloat16 [131072, 2048], P(('island', 'fsdp')), may hold values from -6 to 6
- routes: int32 [131072, 1], P(('island', 'fsdp')), may hold values from 0 to 1; in each aligned block of 512 rows (0 to 511, 512 to 1023, ...) at most 320 rows name the same one
- gains: float32 [131072], P(('island', 'fsdp')), may hold values from 0.25 to 1
Outputs:
- new_base_in: float32 [2, 2048, 2048], P(None, 'fsdp', 'island')
- new_base_out: float32 [2, 1024, 2048], P(None, 'fsdp', 'island')
- new_mom_in: float32 [2, 2048, 2048], P(None, 'fsdp', 'island')
- new_mom_out: float32 [2, 1024, 2048], P(None, 'fsdp', 'island')
- mixed: bfloat16 [131072, 2048], P(('island', 'fsdp'))
The draws below stay inside these ranges and needn't reach their ends.
Inputs may be any that keep to these rules, and one draw needn't show every extreme that they name: `routes`: in the rows of one device at most 320 tokens go to one expert.
All inputs are finite; a program needn't handle non-finite values.
Results may differ from the reference program's by a relative error of at most 0.03.
Values may be sent and summed in bfloat16 or wider, within the bound.
No kernel may reach another device: no remote copies, remote signals or barrier semaphores. Data moves between devices by JAX's collectives and lax.ppermute only.
A program may use at most 128 MiB of HBM per device.

```python
import math
import jax
import jax.numpy as jnp
import numpy as np
from jax import lax

D = 2048
FF = 1024
EXP_WIN = 2
TOK_DEV = 512
CAP = 320
TOKENS = 131072
N_ISLAND = 8


def replica_family(key, salt, rows, cols, fan):
    key = jax.random.fold_in(key, salt)
    key_base = jax.random.fold_in(key, 0)
    key_expo = jax.random.fold_in(key, 1)
    key_noise = jax.random.fold_in(key, 2)
    key_tail = jax.random.fold_in(key, 3)
    key_pair = jax.random.fold_in(key, 5)
    shape_base = (EXP_WIN, rows, cols)
    base = jax.random.normal(key_base, shape_base, jnp.float32)
    base = base * fan ** (-0.5)
    expo = jax.random.randint(key_expo, (EXP_WIN, rows), -12, -7).astype(jnp.int32)
    shape_local = (N_ISLAND, EXP_WIN, rows, cols)
    own = jax.random.normal(key_noise, shape_local, jnp.float32)
    mixture = own
    tails = jnp.exp(0.6 * jax.random.normal(key_tail, shape_local, jnp.float32))
    pairing = jax.random.permutation(key_pair, N_ISLAND)
    column_block = jnp.arange(cols, dtype=jnp.int32) // (cols // N_ISLAND)
    boost = jnp.where(column_block[None, :] == pairing[:, None], 4.0, 1.0)[:, None, None, :]
    delta = mixture * tails * boost * 20.0 * jnp.exp2(expo.astype(jnp.float32))[None, :, :, None]
    return (base, expo, base[None] - delta)


def draw_base_in(key, part):
    return replica_family(key, 11, D, 2 * FF, D)[0]


def draw_exp_in(key, part):
    return replica_family(key, 11, D, 2 * FF, D)[1]


def draw_local_in(key, part):
    return replica_family(key, 11, D, 2 * FF, D)[2].astype(jnp.bfloat16)


def draw_base_out(key, part):
    return replica_family(key, 23, FF, D, FF)[0]


def draw_exp_out(key, part):
    return replica_family(key, 23, FF, D, FF)[1]


def draw_local_out(key, part):
    return replica_family(key, 23, FF, D, FF)[2].astype(jnp.bfloat16)


def block_scale(own_key, extent, shards, least, top_value):
    level, own = 1.0, jax.random.fold_in(own_key, 6)
    for dim, blocks in shards:
        steps = jnp.exp(jax.random.uniform(jax.random.fold_in(own, dim), (blocks,), jnp.float32, least / len(shards), top_value / len(shards)))
        level = level * jnp.repeat(steps, extent[dim] // blocks).reshape([-1 if axis == dim else 1 for axis in range(len(extent))])
    return level


def routed_block(stream_key, own, number, rows, amount, top, most, slope):
    order = jax.random.permutation(stream_key, amount)
    crowded, usual = portions_of(amount, rows * top, most, slope, True), portions_of(amount, rows * top, most, slope, False)
    places = jnp.arange(amount)

    def named(sizes, offset_by):
        used = int((sizes > 0).sum())
        fixed = max(1, used // 4)
        moved = fixed + (places - fixed + offset_by * (used - fixed)) % max(1, amount - fixed)
        return jnp.zeros((amount,), jnp.int32).at[order[jnp.where(places < fixed, places, moved)]].set(jnp.asarray(sizes, jnp.int32))

    sizes = jnp.where(number % 4 == 0, named(crowded, number // 4), named(usual, number - number // 4 - 1))
    mixed = jax.random.permutation(jax.random.fold_in(own, 3), amount)
    donor, receiver = mixed[0:amount // 2 * 2:2], mixed[1:amount // 2 * 2:2]
    slack = jnp.minimum(sizes[donor] - 1, most - sizes[receiver]) // 2
    slack = jnp.where((donor == order[0]) | (receiver == order[0]) | (sizes[receiver] == 0), 0, jnp.maximum(slack, 0))
    moved = jax.random.randint(jax.random.fold_in(own, 4), (amount // 2,), 0, 1 << 20) % (slack + 1)
    sizes = sizes.at[donor].add(-moved).at[receiver].add(moved)
    members = jnp.searchsorted(jnp.cumsum(sizes), jnp.arange(rows * top), side="right").astype(jnp.int32)
    grid = members.reshape(top, rows).T
    grid = grid[jax.random.permutation(jax.random.fold_in(own, 1), rows)]
    offset_by = jax.random.randint(jax.random.fold_in(own, 2), (rows, 1), 0, top)
    return jnp.take_along_axis(grid, (jnp.arange(top)[None, :] + offset_by) % top, axis=1)


def portions_of(amount, total, limit, lean, full):
    portions = [(1 << 20) // math.isqrt(grade ** lean) + 1 for grade in range(1, amount + 1)]
    largest = limit if full else min(limit, max(-(-total // amount), total * portions[0] // sum(portions)))
    least = 1 if total - largest >= amount - 1 else 0
    given, surplus = [largest] + [least] * (amount - 1), total - largest - least * (amount - 1)
    while surplus > 0:
        free = [i for i in range(1, amount) if given[i] < largest] or [i for i in range(1, amount) if given[i] < limit]
        whole, remaining = sum([portions[i] for i in free]), surplus
        for i in free:
            more = min(limit - given[i], max(1, remaining * portions[i] // whole), surplus)
            given[i] = given[i] + more
            surplus = surplus - more
    return np.array(given)


def noise(stream_key, shape, width, limit, shards=(), held_as=jnp.bfloat16):
    drawn = width * jax.random.normal(stream_key, shape, jnp.float32)
    if shards:
        drawn = drawn * block_scale(stream_key, shape, shards, -0.22, 0.18)
    return jnp.clip(drawn, -limit, limit).astype(held_as)


def setup_inputs(seed: int = 0) -> dict:
    splits = jax.random.split(jax.random.key(seed), 12)
    base_in = draw_base_in(jax.random.fold_in(splits[11], 71), 0)
    base_out = draw_base_out(jax.random.fold_in(splits[11], 71), 0)
    local_in = draw_local_in(jax.random.fold_in(splits[11], 71), 0)
    local_out = draw_local_out(jax.random.fold_in(splits[11], 71), 0)
    mom_in = noise(splits[4], (EXP_WIN, D, 2 * FF), 0.02, 0.12, ((1, 32),), jnp.float32)
    mom_out = noise(splits[5], (EXP_WIN, FF, D), 0.02, 0.12, ((1, 32),), jnp.float32)
    exp_in = draw_exp_in(jax.random.fold_in(splits[11], 71), 0)
    exp_out = draw_exp_out(jax.random.fold_in(splits[11], 71), 0)
    tokens = noise(splits[8], (TOKENS, D), 1.0, 6.0, ((0, 256),))
    routes_keys = jax.random.split(jax.random.fold_in(splits[9], 1), TOKENS // TOK_DEV)
    routes_turns = jax.random.permutation(jax.random.fold_in(splits[9], 3), TOKENS // TOK_DEV)
    routes = jax.vmap(lambda own, number: routed_block(jax.random.fold_in(splits[9], 2), own, number, TOK_DEV, EXP_WIN, 1, CAP, 0))(routes_keys, routes_turns).reshape((TOKENS, 1))
    gains = jnp.clip(jnp.exp(math.log(1.0) - 1.3862944 * jax.random.uniform(splits[10], (TOKENS,), jnp.float32) ** block_scale(splits[10], (TOKENS,), ((0, 256),), -0.2, 0.2)), 0.25, 1.0)
    return {"base_in": base_in, "base_out": base_out, "local_in": local_in, "local_out": local_out, "mom_in": mom_in, "mom_out": mom_out, "exp_in": exp_in, "exp_out": exp_out, "tokens": tokens, "routes": routes, "gains": gains}


def outer_step(base, local, moment, expo):
    scale_down = jnp.exp2(-expo.astype(jnp.float32))[None, :, :, None]
    quant = jnp.clip((base[None] - local.astype(jnp.float32)) * scale_down, -127.0, 127.0).astype(jnp.bfloat16)
    total = jnp.sum(quant.astype(jnp.float32), axis=0)
    grad = total * jnp.exp2(expo.astype(jnp.float32))[:, :, None] / N_ISLAND
    new_mom = 0.9 * moment + grad
    new_base = base - 0.7 * (grad + 0.9 * new_mom)
    return new_base, new_mom


def reference(base_in, base_out, local_in, local_out, mom_in, mom_out, exp_in, exp_out, tokens, routes, gains):
    new_base_in, new_mom_in = outer_step(base_in, local_in, mom_in, exp_in)
    new_base_out, new_mom_out = outer_step(base_out, local_out, mom_out, exp_out)
    weights_in = new_base_in.astype(jnp.bfloat16)
    weights_out = new_base_out.astype(jnp.bfloat16)
    blocks = tokens.shape[0] // TOK_DEV

    def one_block(items):
        rows, route_rows, gain_rows = items
        route = route_rows[:, 0]
        positions = jnp.arange(TOK_DEV, dtype=jnp.int32)
        result = jnp.zeros((TOK_DEV, D), jnp.float32)
        for expert in range(EXP_WIN):
            chosen = route == expert
            keys = jnp.where(chosen, positions, positions + TOK_DEV)
            slot_rows = jnp.argsort(keys)[:CAP].astype(jnp.int32)
            count = jnp.sum(chosen.astype(jnp.int32))
            valid = (jnp.arange(CAP, dtype=jnp.int32) < count).astype(jnp.float32)
            picked = rows[slot_rows]
            proj = jnp.dot(picked, weights_in[expert], preferred_element_type=jnp.float32)
            hidden = (jax.nn.silu(proj[:, :FF]) * proj[:, FF:]).astype(jnp.bfloat16)
            outcome = jnp.dot(hidden, weights_out[expert], preferred_element_type=jnp.float32)
            outcome = outcome * (gain_rows[slot_rows] * valid)[:, None]
            result = result.at[slot_rows].add(outcome)
        return result.astype(jnp.bfloat16)

    mixed = lax.map(one_block, (tokens.reshape(blocks, TOK_DEV, D), routes.reshape(blocks, TOK_DEV, 1), gains.reshape(blocks, TOK_DEV)))
    return new_base_in, new_base_out, new_mom_in, new_mom_out, mixed.reshape(blocks * TOK_DEV, D)
```

```python
import jax
import jax.numpy as jnp
from jax import lax
from jax.experimental import pallas as pl
from jax.experimental.pallas import tpu as pltpu
from jax.sharding import Mesh
from jax.sharding import PartitionSpec as P

FF = 1024
CAP = 320
ZH, CORE, ZL, Y, X = 4, 2, 2, 4, 4
AXES = ("zh", "core", "zl", "y", "x")
ISLAND = ("zh", "core")
FSDP = ("zl", "y", "x")
COLS = 256
ROWS_IN, ROWS_OUT = 64, 32
ROWS = ROWS_IN + ROWS_OUT


def shift(size, step):
    return [(i, (i + step) % size) for i in range(size)]


def column_pairs(sign):
    pairs = []
    for zh in range(ZH):
        for core in range(CORE):
            for zl in range(ZL):
                z = (zh * ZL + zl + sign * (1 - 2 * core)) % (ZH * ZL)
                pairs.append(
                    ((zh * CORE + core) * ZL + zl, ((z // ZL) * CORE + core) * ZL + z % ZL)
                )
    return pairs


def quantize(base, local, expo):
    scale_down = jnp.exp2(-expo.astype(jnp.float32))[:, :, None]
    return jnp.clip((base - local[0].astype(jnp.float32)) * scale_down, -127.0, 127.0).astype(
        jnp.bfloat16
    )


def nesterov(base, moment, total, expo, groups):
    grad = total * jnp.exp2(expo.astype(jnp.float32))[:, :, None] / groups
    new_mom = 0.9 * moment + grad
    new_base = base - 0.7 * (grad + 0.9 * new_mom)
    return (new_base, new_mom)


def dot(a, b):
    return jnp.dot(a, b, preferred_element_type=jnp.float32)


def hidden_kernel(place, own, got, gate_m, up_m, gate_o, up_o, out):
    core = place[1]
    for rows, x in ((0, own), (CAP, got)):

        def product(w):
            return sum(
                dot(
                    x[:, zl * 1024 : (zl + 1) * 1024],
                    w[:, 0, zl].reshape(Y * X * ROWS_IN, COLS),
                )
                for zl in range(ZL)
            )

        def half(gate, up):
            return (jax.nn.silu(product(gate)) * product(up)).astype(jnp.bfloat16)

        mine, other = half(gate_m, up_m), half(gate_o, up_o)
        out[rows : rows + CAP, :COLS] = jnp.where(core == 0, mine, other)
        out[rows : rows + CAP, COLS:] = jnp.where(core == 0, other, mine)


def hidden_call(place, own, got, mine, other):
    def block(shift_by):
        return pl.BlockSpec(
            (Y * X, 1, ZL, ROWS_IN, COLS),
            lambda i, s: (0, (s[0] - i - shift_by + ZH) % ZH, 0, 0, 0),
        )

    tokens = pl.BlockSpec((CAP, 2048), lambda i, s: (0, 0))
    return pl.pallas_call(
        hidden_kernel,
        grid_spec=pltpu.PrefetchScalarGridSpec(
            num_scalar_prefetch=1,
            grid=(2,),
            in_specs=[tokens, tokens, block(0), block(2), block(0), block(2)],
            out_specs=pl.BlockSpec((2 * CAP, 2 * COLS), lambda i, s: (0, i)),
        ),
        out_shape=jax.ShapeDtypeStruct((2 * CAP, FF), jnp.bfloat16),
        compiler_params=pltpu.CompilerParams(vmem_limit_bytes=40 * 2**20),
        cost_estimate=pl.CostEstimate(
            flops=2 * 640 * 2048 * 2048, bytes_accessed=12 * 2**20, transcendentals=640 * 1024
        ),
        name="hidden",
    )(place, own, got, mine, mine, other, other)


def outcome_kernel(place, hidden, w_m, w_o, out):
    core = place[1]

    def product(w):
        return sum(
            dot(
                hidden[:, zl * 512 : (zl + 1) * 512],
                w[:, 0, zl].reshape(Y * X * ROWS_OUT, COLS),
            )
            for zl in range(ZL)
        ).astype(jnp.bfloat16)

    mine, other = product(w_m), product(w_o)
    out[:, :COLS] = jnp.where(core == 0, mine, other)
    out[:, COLS:] = jnp.where(core == 0, other, mine)


def outcome_call(place, hidden, part, mine, other):
    block = pl.BlockSpec(
        (Y * X, 1, ZL, ROWS_OUT, COLS), lambda i, s: (0, (s[0] - i + ZH) % ZH, 0, 2, 0)
    )
    return pl.pallas_call(
        outcome_kernel,
        grid_spec=pltpu.PrefetchScalarGridSpec(
            num_scalar_prefetch=1,
            grid=(ZH,),
            in_specs=[pl.BlockSpec((CAP, FF), lambda i, s: (part, 0)), block, block],
            out_specs=pl.BlockSpec((CAP, 2 * COLS), lambda i, s: (0, i)),
        ),
        out_shape=jax.ShapeDtypeStruct((CAP, 2048), jnp.bfloat16),
        compiler_params=pltpu.CompilerParams(vmem_limit_bytes=40 * 2**20),
        cost_estimate=pl.CostEstimate(
            flops=2 * 320 * 1024 * 2048, bytes_accessed=6 * 2**20, transcendentals=0
        ),
        name="outcome",
    )(place, hidden, mine, other)


def place_kernel(put_own, put_got, own, got, gains, out):
    out[...] = ((dot(put_own[...], own[...]) + dot(put_got[...], got[...])) * gains[...]).astype(
        jnp.bfloat16
    )


def place_call(put_own, put_got, own, got, gains):
    rows = put_own.shape[0]
    put = pl.BlockSpec((rows, CAP), lambda i: (0, 0))
    values = pl.BlockSpec((CAP, 512), lambda i: (0, i))
    return pl.pallas_call(
        place_kernel,
        grid=(4,),
        in_specs=[put, put, values, values, pl.BlockSpec((rows, 1), lambda i: (0, 0))],
        out_specs=pl.BlockSpec((rows, 512), lambda i: (0, i)),
        out_shape=jax.ShapeDtypeStruct((rows, 2048), jnp.bfloat16),
        compiler_params=pltpu.CompilerParams(vmem_limit_bytes=40 * 2**20),
        cost_estimate=pl.CostEstimate(
            flops=2 * 512 * 640 * 2048, bytes_accessed=5 * 2**20, transcendentals=0
        ),
        name="place",
    )(put_own, put_got, own, got, gains)


def body(
    base_in, base_out, local_in, local_out, mom_in, mom_out, exp_in, exp_out, tokens, routes, gains
):
    zh, core, zl = lax.axis_index("zh"), lax.axis_index("core"), lax.axis_index("zl")
    block = zh * CORE + core
    scalars = jnp.stack([zh, core]).astype(jnp.int32)

    quant = jnp.concatenate(
        [quantize(base_in, local_in, exp_in), quantize(base_out, local_out, exp_out)], axis=1
    ).reshape(2, ROWS, ZH, CORE, COLS)
    keep = lax.dynamic_index_in_dim(quant, core, 3, keepdims=False)
    give = lax.dynamic_index_in_dim(quant, 1 - core, 3, keepdims=False)
    pair = keep.astype(jnp.float32) + lax.ppermute(give, "core", shift(CORE, 1)).astype(
        jnp.float32
    )
    pair_sent = pair.astype(jnp.bfloat16)
    total = lax.dynamic_index_in_dim(pair, zh, 2, keepdims=False)
    for step in range(1, ZH):
        sent = lax.dynamic_index_in_dim(pair_sent, (zh + step) % ZH, 2, keepdims=False)
        total = total + lax.ppermute(sent, "zh", shift(ZH, step)).astype(jnp.float32)

    def own(whole):
        return lax.dynamic_slice_in_dim(whole, block * COLS, COLS, 2)

    groups = ZH * CORE
    new_base_in, new_mom_in = nesterov(
        own(base_in), own(mom_in), total[:, :ROWS_IN], exp_in, groups
    )
    new_base_out, new_mom_out = nesterov(
        own(base_out), own(mom_out), total[:, ROWS_IN:], exp_out, groups
    )
    weights = jnp.concatenate([new_base_in, new_base_out], axis=1).astype(jnp.bfloat16)

    kept = lax.dynamic_index_in_dim(weights, zl, 0, keepdims=False)
    given = lax.dynamic_index_in_dim(weights, 1 - zl, 0, keepdims=False)
    taken = lax.ppermute(given, "zl", shift(ZL, 1))
    both = jnp.stack([jnp.where(zl == 0, kept, taken), jnp.where(zl == 0, taken, kept)])
    column = jnp.stack(
        [both] + [lax.ppermute(both, "zh", shift(ZH, step)) for step in range(1, ZH)]
    )
    mine = lax.all_gather(column, ("y", "x"), axis=0, tiled=False)
    mine = mine.reshape(Y * X, ZH, ZL, ROWS, COLS)
    other = lax.ppermute(mine, "core", shift(CORE, 1))

    route = routes[:, 0]
    rank_of = []
    for named in (zl, 1 - zl):
        chosen = route == named
        rank = jnp.cumsum(chosen.astype(jnp.int32)) - 1
        rank_of.append(jnp.where(chosen, rank, -1))
    slots = jnp.arange(CAP, dtype=jnp.int32)
    pick_own, pick_got = [(slots[:, None] == r[None, :]).astype(jnp.bfloat16) for r in rank_of]
    put_own, put_got = [(r[:, None] == slots[None, :]).astype(jnp.bfloat16) for r in rank_of]
    tokens_own = dot(pick_own, tokens).astype(jnp.bfloat16)
    tokens_sent = dot(pick_got, tokens).astype(jnp.bfloat16)
    tokens_sent, _ = lax.optimization_barrier((tokens_sent, column))
    column_axes = ("zh", "core", "zl")
    tokens_got = lax.ppermute(tokens_sent, column_axes, column_pairs(1))

    hidden = hidden_call(scalars, tokens_own, tokens_got, mine, other)
    result_got = outcome_call(scalars, hidden, 1, mine, other)
    result_back = lax.ppermute(result_got, column_axes, column_pairs(-1))
    result_own = outcome_call(scalars, hidden, 0, mine, other)
    mixed = place_call(put_own, put_got, result_own, result_back, gains[:, None])
    return (new_base_in, new_base_out, new_mom_in, new_mom_out, mixed)


def solution(mesh):
    split = Mesh(mesh.devices.reshape(ZH, CORE, ZL, Y, X), AXES)
    in_specs = (
        P(None, FSDP, None),
        P(None, FSDP, None),
        P(ISLAND, None, FSDP, None),
        P(ISLAND, None, FSDP, None),
        P(None, FSDP, None),
        P(None, FSDP, None),
        P(None, FSDP),
        P(None, FSDP),
        P(ISLAND + FSDP, None),
        P(ISLAND + FSDP, None),
        P(ISLAND + FSDP),
    )
    out_specs = (
        P(None, FSDP, ISLAND),
        P(None, FSDP, ISLAND),
        P(None, FSDP, ISLAND),
        P(None, FSDP, ISLAND),
        P(ISLAND + FSDP, None),
    )
    return jax.shard_map(body, mesh=split, in_specs=in_specs, out_specs=out_specs, check_vma=False)
```

```python
import jax
import jax.numpy as jnp
import numpy as np
from jax import lax
from jax.experimental import pallas as pl
from jax.experimental.pallas import tpu as pltpu
from jax.sharding import Mesh
from jax.sharding import PartitionSpec as P

D = 2048
FF = 1024
CAP = 320
ZH, CORE, ZL, Y, X = 4, 2, 2, 4, 4
AXES = ("zh", "core", "zl", "y", "x")
ISLAND = ("zh", "core")
FSDP = ("zl", "y", "x")
COLUMN = ("zh", "core", "zl")
GROUPS = ZH * CORE
COLS = 256
ROWS_IN, ROWS_OUT = 64, 32
ROWS = ROWS_IN + ROWS_OUT
PIECES = Y * X
HALF = PIECES // 2
SETS = 2
BF16, F32 = jnp.bfloat16, jnp.float32

MASKS = ((1, 3), (3, 1))
REACH = tuple((0, a, b, a ^ b) for a, b in MASKS)


def piece_table():
    table = np.zeros((CORE, Y, X, 2, PIECES), np.int32)
    for core in range(CORE):
        for y in range(Y):
            for x in range(X):
                for p in range(PIECES):
                    first, second = REACH[core][p % 4], REACH[core][p // 4]
                    table[core, y, x, 0, p] = (y ^ second) * X + (x ^ first)
                    table[core, y, x, 1, p] = (y ^ first) * X + (x ^ second)
    return table


def shift(size, step):
    return [(i, (i + step) % size) for i in range(size)]


def flip_pairs(turn):
    return [
        (core * 4 + i, core * 4 + (i ^ MASKS[core][turn])) for core in range(CORE) for i in range(4)
    ]


def column_pairs(sign, swap):
    pairs = []
    for zh in range(ZH):
        for core in range(CORE):
            for zl in range(ZL):
                z = (zh * ZL + zl + sign * (1 - 2 * core)) % (ZH * ZL)
                sender = core ^ swap
                pairs.append(
                    ((zh * CORE + sender) * ZL + zl, ((z // ZL) * CORE + core) * ZL + z % ZL)
                )
    return pairs


def dot(a, b):
    return jnp.dot(a, b, preferred_element_type=F32)


def params(mib=48):
    return pltpu.CompilerParams(vmem_limit_bytes=mib * 2**20)


def row_exponents(expo, rows):
    eye = lax.broadcasted_iota(jnp.int32, (rows, rows), 0) == lax.broadcasted_iota(
        jnp.int32, (rows, rows), 1
    )
    lines = [jnp.where(eye, expo[e : e + 1, :].astype(F32), 0.0) for e in range(2)]
    return jnp.stack([jnp.sum(line, axis=1, keepdims=True) for line in lines])


def give_kernel(
    place, b_in, l_in, e_in, b_out, l_out, e_out, m_in, m_out,
    given, kept, ob_in, ob_out, om_in, om_out, sems,
):
    zh, core = place[0], place[1]
    mine = pl.ds(pl.multiple_of((zh * CORE + core) * COLS, COLS), COLS)
    copies = [
        pltpu.make_async_copy(whole.at[:, :, mine], out, sems.at[i])
        for i, (whole, out) in enumerate(((m_in, om_in), (m_out, om_out)))
    ]
    for copy in copies:
        copy.start()
    ob_in[...] = b_in[:, :, mine]
    ob_out[...] = b_out[:, :, mine]
    for base, local, expo, rows, first in (
        (b_in, l_in, e_in, ROWS_IN, 0),
        (b_out, l_out, e_out, ROWS_OUT, ROWS_IN),
    ):
        scale = jnp.exp2(-row_exponents(expo, rows))
        for step in range(ZH):
            for out, side in ((given, 1 - core), (kept, core)):
                column = (((zh + step) % ZH) * CORE + side) * COLS
                at = pl.ds(pl.multiple_of(column, COLS), COLS)
                quant = (base[:, :, at] - local[0, :, :, at].astype(F32)) * scale
                out[step, :, first : first + rows] = jnp.clip(quant, -127.0, 127.0).astype(BF16)
    for copy in copies:
        copy.wait()


def give_call(place, arrays, moments):
    vmem, anywhere = pl.BlockSpec(memory_space=pltpu.VMEM), pl.BlockSpec(memory_space=pl.ANY)
    own = [jax.ShapeDtypeStruct((2, r, COLS), F32) for r in (ROWS_IN, ROWS_OUT) * 2]
    return pl.pallas_call(
        give_kernel,
        in_specs=[pl.BlockSpec(memory_space=pltpu.SMEM)] + [vmem] * 6 + [anywhere] * 2,
        out_specs=[vmem] * 6,
        out_shape=[jax.ShapeDtypeStruct((ZH, 2, ROWS, COLS), BF16)] * 2 + own,
        scratch_shapes=[pltpu.SemaphoreType.DMA((2,))],
        compiler_params=params(60),
        cost_estimate=pl.CostEstimate(flops=10**6, bytes_accessed=4 * 2**20, transcendentals=0),
        name="give",
    )(place, *arrays, *moments)


def pair_kernel(kept, taken, own, *sent):
    for step, out in enumerate((own,) + sent):
        out[...] = (kept[step].astype(F32) + taken[step].astype(F32)).astype(out.dtype)


def pair_call(kept, taken):
    vmem = pl.BlockSpec(memory_space=pltpu.VMEM)
    return pl.pallas_call(
        pair_kernel,
        in_specs=[vmem] * 2,
        out_specs=[vmem] * ZH,
        out_shape=[jax.ShapeDtypeStruct((2, ROWS, COLS), F32)]
        + [jax.ShapeDtypeStruct((2, ROWS, COLS), BF16)] * (ZH - 1),
        compiler_params=params(16),
        cost_estimate=pl.CostEstimate(flops=10**6, bytes_accessed=2 * 2**20, transcendentals=0),
        name="pair",
    )(kept, taken)


def step_kernel(
    place, own, r1, r2, r3, b_in, m_in, e_in, b_out, m_out, e_out,
    nb_in, nb_out, nm_in, nm_out, kept, given, weights,
):
    total = own[...] + r1[...].astype(F32) + r2[...].astype(F32) + r3[...].astype(F32)

    def nesterov(base, moment, part, expo):
        grad = part * jnp.exp2(expo) / GROUPS
        new_mom = 0.9 * moment + grad
        return base - 0.7 * (grad + 0.9 * new_mom), new_mom

    nb_in[...], nm_in[...] = nesterov(
        b_in[...], m_in[...], total[:, :ROWS_IN], row_exponents(e_in, ROWS_IN)
    )
    nb_out[...], nm_out[...] = nesterov(
        b_out[...], m_out[...], total[:, ROWS_IN:], row_exponents(e_out, ROWS_OUT)
    )
    weights[:, :ROWS_IN] = nb_in[...].astype(BF16)
    weights[:, ROWS_IN:] = nb_out[...].astype(BF16)
    kept[...] = weights[place[2]]
    given[...] = weights[1 - place[2]]


def step_call(place, own, received, base_in, mom_in, exp_in, base_out, mom_out, exp_out):
    vmem = pl.BlockSpec(memory_space=pltpu.VMEM)
    new = [(2, r, COLS) for r in (ROWS_IN, ROWS_OUT, ROWS_IN, ROWS_OUT)]
    return pl.pallas_call(
        step_kernel,
        in_specs=[pl.BlockSpec(memory_space=pltpu.SMEM)] + [vmem] * 10,
        out_specs=[vmem] * 6,
        out_shape=[jax.ShapeDtypeStruct(shape, F32) for shape in new]
        + [jax.ShapeDtypeStruct((ROWS, COLS), BF16)] * 2,
        scratch_shapes=[pltpu.VMEM((2, ROWS, COLS), BF16)],
        compiler_params=params(16),
        cost_estimate=pl.CostEstimate(flops=10**6, bytes_accessed=2 * 2**20, transcendentals=0),
        name="step",
    )(place, own, *received, base_in, mom_in, exp_in, base_out, mom_out, exp_out)


def load_pieces(table, pieces, held, sems, colour, rows):
    copies = []
    for p in range(PIECES):
        copies.append(
            pltpu.make_async_copy(
                pieces[colour * 4 + p // 4].at[p % 4, :, :, rows],
                held.at[colour, :, :, table[4 + colour * PIECES + p]],
                sems.at[colour, p],
            )
        )
    for copy in copies:
        copy.start()
    return copies


def hidden_kernel(table, *refs):
    sets, pieces, (out, x, held, x_sems, sems) = refs[:SETS], refs[SETS : SETS + 8], refs[SETS + 8 :]
    zh, zl = table[0], table[2]
    rows = pl.ds(0, ROWS_IN)
    loads = [pltpu.make_async_copy(sets[i], x.at[i], x_sems.at[i]) for i in range(SETS)]
    loads[0].start()
    copies = [load_pieces(table, pieces, held, sems, 0, rows)]
    loads[1].start()
    copies.append(load_pieces(table, pieces, held, sems, 1, rows))
    gates = (zh // 2, jnp.where((zh == 0) | (zh == 3), 1, 0))
    for colour in range(2):
        for copy in copies[colour]:
            copy.wait()
        for i in range(SETS):
            if colour == 0:
                loads[i].wait()

            def product(k):
                return sum(
                    dot(
                        x[i, :, part * 1024 : (part + 1) * 1024],
                        held[colour, k, part ^ zl].reshape(PIECES * ROWS_IN, COLS),
                    )
                    for part in range(ZL)
                )

            gate, up = product(gates[colour]), product(1 - gates[colour])
            out[i * CAP : (i + 1) * CAP, colour * COLS : (colour + 1) * COLS] = (
                jax.nn.silu(gate) * up
            ).astype(BF16)


SMALL = pl.CostEstimate(flops=10**6, bytes_accessed=10**5, transcendentals=0)


def hidden_call(table, sets, pieces):
    vmem, anywhere = pl.BlockSpec(memory_space=pltpu.VMEM), pl.BlockSpec(memory_space=pl.ANY)
    return pl.pallas_call(
        hidden_kernel,
        in_specs=[pl.BlockSpec(memory_space=pltpu.SMEM)] + [anywhere] * (SETS + 8),
        out_specs=vmem,
        out_shape=jax.ShapeDtypeStruct((SETS * CAP, FF // 2), BF16),
        scratch_shapes=[
            pltpu.VMEM((SETS, CAP, D), BF16),
            pltpu.VMEM((2, 2, ZL, PIECES, ROWS_IN, COLS), BF16),
            pltpu.SemaphoreType.DMA((SETS,)),
            pltpu.SemaphoreType.DMA((2, PIECES)),
        ],
        compiler_params=params(24),
        cost_estimate=pl.CostEstimate(flops=10**6, bytes_accessed=8 * 2**20, transcendentals=0),
        name="hidden",
    )(table, *sets, *pieces)


def outcome_kernel(table, made, got, *refs):
    pieces, outs, (held, sems) = refs[:8], refs[8 : 8 + SETS], refs[8 + SETS :]
    zh, core = table[0], table[1]
    rows = pl.ds(ROWS_IN, ROWS_OUT)
    copies = [load_pieces(table, pieces, held, sems, colour, rows) for colour in range(2)]
    for colour in range(2):
        for copy in copies[colour]:
            copy.wait()
    for i, out in enumerate(outs):
        halves = ((made, i, core), (got, i ^ 1, 1 - core))
        for column in range(ZH):
            k = (zh - column + ZH) % ZH
            total = 0.0
            for colour in range(2):
                part = ((zh + colour) % 2) ^ table[2]
                for hidden, at, side in halves:
                    w = held[k % 2, k // 2, part, pl.ds(side * HALF, HALF)]
                    total = total + dot(
                        hidden[at * CAP : (at + 1) * CAP, colour * COLS : (colour + 1) * COLS],
                        w.reshape(HALF * ROWS_OUT, COLS),
                    )
            out[:, column * COLS : (column + 1) * COLS] = total.astype(BF16)


def outcome_call(table, made, got, pieces):
    vmem, anywhere = pl.BlockSpec(memory_space=pltpu.VMEM), pl.BlockSpec(memory_space=pl.ANY)
    return pl.pallas_call(
        outcome_kernel,
        in_specs=[pl.BlockSpec(memory_space=pltpu.SMEM)] + [vmem] * 2 + [anywhere] * 8,
        out_specs=[vmem] * SETS,
        out_shape=[jax.ShapeDtypeStruct((CAP, D // 2), BF16)] * SETS,
        scratch_shapes=[
            pltpu.VMEM((2, 2, ZL, PIECES, ROWS_OUT, COLS), BF16),
            pltpu.SemaphoreType.DMA((2, PIECES)),
        ],
        compiler_params=params(16),
        cost_estimate=pl.CostEstimate(flops=10**6, bytes_accessed=4 * 2**20, transcendentals=0),
        name="outcome",
    )(table, made, got, *pieces)


def put_kernel(first, table, put, same, cross, gains, *refs):
    out = refs[-1]
    core = table[1]
    for values, side in ((same, core), (cross, 1 - core)):
        at = pl.ds(pl.multiple_of(side * COLS, COLS), COLS)
        rows = (dot(put[...], values[...]) * gains[...]).astype(BF16)
        out[:, at] = rows if first else rows + refs[0][:, at]


def put_call(table, put, same, cross, gains, before=None):
    rows = put.shape[0]
    values = pl.BlockSpec((CAP, COLS), lambda i, s: (0, i))
    block = pl.BlockSpec((rows, 2 * COLS), lambda i, s: (0, i))
    more = [] if before is None else [before]

    def kernel(*refs):
        put_kernel(before is None, *refs)

    return pl.pallas_call(
        kernel,
        grid_spec=pltpu.PrefetchScalarGridSpec(
            num_scalar_prefetch=1,
            grid=(ZH,),
            in_specs=[
                pl.BlockSpec((rows, CAP), lambda i, s: (0, 0)),
                values,
                values,
                pl.BlockSpec((rows, 1), lambda i, s: (0, 0)),
            ]
            + [block] * len(more),
            out_specs=block,
        ),
        out_shape=jax.ShapeDtypeStruct((rows, D), BF16),
        compiler_params=params(16),
        cost_estimate=SMALL,
        name="put",
    )(table, put, same, cross, gains, *more)


def body(
    base_in, base_out, local_in, local_out, mom_in, mom_out, exp_in, exp_out, tokens, routes, gains
):
    zh, core, zl = lax.axis_index("zh"), lax.axis_index("core"), lax.axis_index("zl")
    y, x = lax.axis_index("y"), lax.axis_index("x")
    place = jnp.stack([zh, core, zl, zl]).astype(jnp.int32)
    spots = jnp.asarray(piece_table().reshape(CORE * Y * X, 2 * PIECES))
    spots = lax.dynamic_index_in_dim(spots, (core * Y + y) * X + x, 0, keepdims=False)
    table = jnp.concatenate([place, spots])

    given, kept, b_in, b_out, m_in, m_out = give_call(
        place, (base_in, local_in, exp_in, base_out, local_out, exp_out), (mom_in, mom_out)
    )
    own, *sent = pair_call(kept, lax.ppermute(given, "core", shift(CORE, 1)))
    received = [lax.ppermute(sent[s - 1], "zh", shift(ZH, s)) for s in range(1, ZH)]
    new_base_in, new_base_out, new_mom_in, new_mom_out, kept, given = step_call(
        place, own, received, b_in, m_in, exp_in, b_out, m_out, exp_out
    )

    routes, _ = lax.optimization_barrier((routes, own))
    route = routes[:, 0]
    rank_of = []
    for named in (zl, 1 - zl):
        chosen = route == named
        rank = jnp.cumsum(chosen.astype(jnp.int32)) - 1
        rank_of.append(jnp.where(chosen, rank, -1))
    slots = jnp.arange(CAP, dtype=jnp.int32)
    pick_own, pick_got = [(slots[:, None] == r[None, :]).astype(BF16) for r in rank_of]
    put_own, put_got = [(r[:, None] == slots[None, :]).astype(BF16) for r in rank_of]
    tokens_own = dot(pick_own, tokens).astype(BF16)
    tokens_sent = dot(pick_got, tokens).astype(BF16)
    other_own = lax.ppermute(tokens_own, "core", shift(CORE, 1))

    taken = lax.ppermute(given, "zl", shift(ZL, 1))
    kept, taken, tokens_sent, other_own = lax.optimization_barrier(
        (kept, taken, tokens_sent, other_own)
    )
    both = jnp.stack([kept, taken])
    column = [both] + [lax.ppermute(both, "zh", shift(ZH, s)) for s in range(1, ZH)]
    *column, tokens_sent = lax.optimization_barrier((*column, tokens_sent))

    tokens_got = lax.ppermute(tokens_sent, COLUMN, column_pairs(1, 0))
    held = [jnp.stack([column[c], column[c + 2]])[None] for c in (0, 1)]

    def exchange(arrays, axes, turn):
        return [
            lax.ppermute(a, ("core", axis), flip_pairs(turn)) for a, axis in zip(arrays, axes)
        ]

    for turn in range(2):
        held = [jnp.concatenate(pair) for pair in zip(held, exchange(held, ("x", "y"), turn))]
    first = exchange(held, ("y", "x"), 0)
    second = exchange(held, ("y", "x"), 1)
    third = exchange(first, ("y", "x"), 1)
    pieces = [part[c] for c in range(2) for part in (held, first, second, third)]
    other_got = lax.ppermute(tokens_got, "core", shift(CORE, 1))

    made = hidden_call(table, (other_got, tokens_got), pieces)
    got = lax.ppermute(made, "core", shift(CORE, 1))
    other_own, tokens_own, _ = lax.optimization_barrier((other_own, tokens_own, made))
    near = hidden_call(table, (other_own, tokens_own), pieces)
    far_other, far_mine = outcome_call(table, made, got, pieces)
    near, far_other, far_mine = lax.optimization_barrier((near, far_other, far_mine))
    back_same = lax.ppermute(far_mine, COLUMN, column_pairs(-1, 0))
    back_cross = lax.ppermute(far_other, COLUMN, column_pairs(-1, 1))
    near_got = lax.ppermute(near, "core", shift(CORE, 1))
    near_other, near_mine = outcome_call(table, near, near_got, pieces)
    near_cross = lax.ppermute(near_other, "core", shift(CORE, 1))
    scale = gains[:, None]
    mixed = put_call(table, put_own, near_mine, near_cross, scale)
    mixed = put_call(table, put_got, back_same, back_cross, scale, mixed)
    return (new_base_in, new_base_out, new_mom_in, new_mom_out, mixed)


def solution(mesh):
    split = Mesh(mesh.devices.reshape(ZH, CORE, ZL, Y, X), AXES)
    in_specs = (
        P(None, FSDP, None),
        P(None, FSDP, None),
        P(ISLAND, None, FSDP, None),
        P(ISLAND, None, FSDP, None),
        P(None, FSDP, None),
        P(None, FSDP, None),
        P(None, FSDP),
        P(None, FSDP),
        P(ISLAND + FSDP, None),
        P(ISLAND + FSDP, None),
        P(ISLAND + FSDP),
    )
    out_specs = (
        P(None, FSDP, ISLAND),
        P(None, FSDP, ISLAND),
        P(None, FSDP, ISLAND),
        P(None, FSDP, ISLAND),
        P(ISLAND + FSDP, None),
    )
    return jax.shard_map(body, mesh=split, in_specs=in_specs, out_specs=out_specs, check_vma=False)
```

```python
import functools

import jax
import jax.numpy as jnp
import numpy as np
from jax import lax
from jax.experimental import pallas as pl
from jax.experimental.pallas import tpu as pltpu
from jax.sharding import Mesh
from jax.sharding import PartitionSpec as P

D = 2048
FF = 1024
CAP = 320
ZH, CORE, ZL, Y, X = 4, 2, 2, 4, 4
AXES = ("zh", "core", "zl", "y", "x")
ISLAND = ("zh", "core")
FSDP = ("zl", "y", "x")
COLUMN = ("zh", "core", "zl")
GROUPS = ZH * CORE
COLS = 256
ROWS_IN, ROWS_OUT = 64, 32
ROWS = ROWS_IN + ROWS_OUT
PIECES = Y * X
HALF = PIECES // 2
SETS = 2
BF16, F32 = jnp.bfloat16, jnp.float32

MASKS = ((1, 3), (3, 1))
REACH = tuple((0, a, b, a ^ b) for a, b in MASKS)


def piece_table():
    table = np.zeros((CORE, Y, X, 2, PIECES), np.int32)
    for core in range(CORE):
        for y in range(Y):
            for x in range(X):
                for p in range(PIECES):
                    first, second = REACH[core][p % 4], REACH[core][p // 4]
                    table[core, y, x, 0, p] = (y ^ second) * X + (x ^ first)
                    table[core, y, x, 1, p] = (y ^ first) * X + (x ^ second)
    return table


def shift(size, step):
    return [(i, (i + step) % size) for i in range(size)]


def flip_pairs(turn):
    return [
        (core * 4 + i, core * 4 + (i ^ MASKS[core][turn])) for core in range(CORE) for i in range(4)
    ]


def column_pairs(sign, swap):
    pairs = []
    for zh in range(ZH):
        for core in range(CORE):
            for zl in range(ZL):
                z = (zh * ZL + zl + sign * (1 - 2 * core)) % (ZH * ZL)
                sender = core ^ swap
                pairs.append(
                    ((zh * CORE + sender) * ZL + zl, ((z // ZL) * CORE + core) * ZL + z % ZL)
                )
    return pairs


def dot(a, b):
    return jnp.dot(a, b, preferred_element_type=F32)


def params(mib=48):
    return pltpu.CompilerParams(vmem_limit_bytes=mib * 2**20)


def column_of(line):
    size = line.shape[1]
    eye = lax.broadcasted_iota(jnp.int32, (size, size), 0) == lax.broadcasted_iota(
        jnp.int32, (size, size), 1
    )
    return jnp.sum(jnp.where(eye, line, 0.0), axis=1, keepdims=True)


def row_exponents(expo):
    return jnp.stack([column_of(expo[e : e + 1, :].astype(F32)) for e in range(2)])


def give_kernel(
    place, b_in, l_in, e_in, b_out, l_out, e_out, m_in, m_out,
    given, kept, ob_in, ob_out, om_in, om_out, sems,
):
    zh, core = place[0], place[1]
    mine = pl.ds(pl.multiple_of((zh * CORE + core) * COLS, COLS), COLS)
    copies = [
        pltpu.make_async_copy(whole.at[:, :, mine], out, sems.at[i])
        for i, (whole, out) in enumerate(((m_in, om_in), (m_out, om_out)))
    ]
    for copy in copies:
        copy.start()
    ob_in[...] = b_in[:, :, mine]
    ob_out[...] = b_out[:, :, mine]
    for base, local, expo, rows, first in (
        (b_in, l_in, e_in, ROWS_IN, 0),
        (b_out, l_out, e_out, ROWS_OUT, ROWS_IN),
    ):
        scale = jnp.exp2(-row_exponents(expo))
        for step in range(ZH):
            for out, side in ((given, 1 - core), (kept, core)):
                column = (((zh + step) % ZH) * CORE + side) * COLS
                at = pl.ds(pl.multiple_of(column, COLS), COLS)
                quant = (base[:, :, at] - local[0, :, :, at].astype(F32)) * scale
                out[step, :, first : first + rows] = jnp.clip(quant, -127.0, 127.0).astype(BF16)
    for copy in copies:
        copy.wait()


def give_call(place, arrays, moments):
    vmem, anywhere = pl.BlockSpec(memory_space=pltpu.VMEM), pl.BlockSpec(memory_space=pl.ANY)
    own = [jax.ShapeDtypeStruct((2, r, COLS), F32) for r in (ROWS_IN, ROWS_OUT) * 2]
    return pl.pallas_call(
        give_kernel,
        in_specs=[pl.BlockSpec(memory_space=pltpu.SMEM)] + [vmem] * 6 + [anywhere] * 2,
        out_specs=[vmem] * 6,
        out_shape=[jax.ShapeDtypeStruct((ZH, 2, ROWS, COLS), BF16)] * 2 + own,
        scratch_shapes=[pltpu.SemaphoreType.DMA((2,))],
        compiler_params=params(60),
        cost_estimate=pl.CostEstimate(flops=10**6, bytes_accessed=4 * 2**20, transcendentals=0),
        name="give",
    )(place, *arrays, *moments)


def pair_kernel(kept, taken, own, *sent):
    for step, out in enumerate((own,) + sent):
        out[...] = (kept[step].astype(F32) + taken[step].astype(F32)).astype(out.dtype)


def pair_call(kept, taken):
    vmem = pl.BlockSpec(memory_space=pltpu.VMEM)
    return pl.pallas_call(
        pair_kernel,
        in_specs=[vmem] * 2,
        out_specs=[vmem] * ZH,
        out_shape=[jax.ShapeDtypeStruct((2, ROWS, COLS), F32)]
        + [jax.ShapeDtypeStruct((2, ROWS, COLS), BF16)] * (ZH - 1),
        compiler_params=params(16),
        cost_estimate=pl.CostEstimate(flops=10**6, bytes_accessed=2 * 2**20, transcendentals=0),
        name="pair",
    )(kept, taken)


def step_kernel(
    place, own, r1, r2, r3, b_in, m_in, e_in, b_out, m_out, e_out,
    nb_in, nb_out, nm_in, nm_out, kept, given, weights,
):
    total = own[...] + r1[...].astype(F32) + r2[...].astype(F32) + r3[...].astype(F32)

    def nesterov(base, moment, part, expo):
        grad = part * jnp.exp2(expo) / GROUPS
        new_mom = 0.9 * moment + grad
        return base - 0.7 * (grad + 0.9 * new_mom), new_mom

    nb_in[...], nm_in[...] = nesterov(
        b_in[...], m_in[...], total[:, :ROWS_IN], row_exponents(e_in)
    )
    nb_out[...], nm_out[...] = nesterov(
        b_out[...], m_out[...], total[:, ROWS_IN:], row_exponents(e_out)
    )
    weights[:, :ROWS_IN] = nb_in[...].astype(BF16)
    weights[:, ROWS_IN:] = nb_out[...].astype(BF16)
    kept[...] = weights[place[2]]
    given[...] = weights[1 - place[2]]


def step_call(place, own, received, base_in, mom_in, exp_in, base_out, mom_out, exp_out):
    vmem = pl.BlockSpec(memory_space=pltpu.VMEM)
    new = [(2, r, COLS) for r in (ROWS_IN, ROWS_OUT, ROWS_IN, ROWS_OUT)]
    return pl.pallas_call(
        step_kernel,
        in_specs=[pl.BlockSpec(memory_space=pltpu.SMEM)] + [vmem] * 10,
        out_specs=[vmem] * 6,
        out_shape=[jax.ShapeDtypeStruct(shape, F32) for shape in new]
        + [jax.ShapeDtypeStruct((ROWS, COLS), BF16)] * 2,
        scratch_shapes=[pltpu.VMEM((2, ROWS, COLS), BF16)],
        compiler_params=params(16),
        cost_estimate=pl.CostEstimate(flops=10**6, bytes_accessed=2 * 2**20, transcendentals=0),
        name="step",
    )(place, own, *received, base_in, mom_in, exp_in, base_out, mom_out, exp_out)


def load_pieces(table, pieces, held, sems, colour, rows):
    copies = []
    for p in range(PIECES):
        copies.append(
            pltpu.make_async_copy(
                pieces[colour * 4 + p // 4].at[p % 4, :, :, rows],
                held.at[colour, :, :, table[4 + colour * PIECES + p]],
                sems.at[colour, p],
            )
        )
    for copy in copies:
        copy.start()
    return copies


def hidden_kernel(parts, table, *refs):
    sets, pieces, outs, (x, held, x_sems, sems) = (
        refs[:SETS],
        refs[SETS : SETS + 8],
        refs[SETS + 8 : -4],
        refs[-4:],
    )
    zh, zl = table[0], table[2]
    rows = pl.ds(0, ROWS_IN)
    loads = [pltpu.make_async_copy(sets[i], x.at[i], x_sems.at[i]) for i in range(SETS)]
    loads[0].start()
    copies = [load_pieces(table, pieces, held, sems, 0, rows)]
    loads[1].start()
    copies.append(load_pieces(table, pieces, held, sems, 1, rows))
    gates = (zh // 2, jnp.where((zh == 0) | (zh == 3), 1, 0))
    for colour in range(2):
        for copy in copies[colour]:
            copy.wait()
        for i in range(SETS):
            if colour == 0:
                loads[i].wait()

            def product(k):
                return sum(
                    dot(
                        x[i, :, part * 1024 : (part + 1) * 1024],
                        held[colour, k, part ^ zl].reshape(PIECES * ROWS_IN, COLS),
                    )
                    for part in range(ZL)
                )

            gate, up = product(gates[colour]), product(1 - gates[colour])
            value = (jax.nn.silu(gate) * up).astype(BF16)
            at = slice(colour * COLS, (colour + 1) * COLS)
            outs[0][i * CAP : (i + 1) * CAP, at] = value
            for part in range(parts):
                step = CAP // parts
                outs[1 + i * parts + part][:, at] = value[part * step : (part + 1) * step]


SMALL = pl.CostEstimate(flops=10**3, bytes_accessed=10**3, transcendentals=0)
LARGE = pl.CostEstimate(flops=10**9, bytes_accessed=6 * 2**20, transcendentals=0)


def hidden_call(table, sets, pieces, parts):
    vmem, anywhere = pl.BlockSpec(memory_space=pltpu.VMEM), pl.BlockSpec(memory_space=pl.ANY)
    return pl.pallas_call(
        functools.partial(hidden_kernel, parts),
        in_specs=[pl.BlockSpec(memory_space=pltpu.SMEM)] + [anywhere] * (SETS + 8),
        out_specs=[vmem] * (1 + SETS * parts),
        out_shape=[jax.ShapeDtypeStruct((SETS * CAP, FF // 2), BF16)]
        + [jax.ShapeDtypeStruct((CAP // parts, FF // 2), BF16)] * (SETS * parts),
        scratch_shapes=[
            pltpu.VMEM((SETS, CAP, D), BF16),
            pltpu.VMEM((2, 2, ZL, PIECES, ROWS_IN, COLS), BF16),
            pltpu.SemaphoreType.DMA((SETS,)),
            pltpu.SemaphoreType.DMA((2, PIECES)),
        ],
        compiler_params=params(24),
        cost_estimate=SMALL,
        name="hidden",
    )(table, *sets, *pieces)


def outcome_kernel(table, made, got0, got1, *refs):
    pieces, outs, (held, sems) = refs[:8], refs[8:-2], refs[-2:]
    zh, core = table[0], table[1]
    rows = pl.ds(ROWS_IN, ROWS_OUT)
    copies = [load_pieces(table, pieces, held, sems, colour, rows) for colour in range(2)]
    for colour in range(2):
        for copy in copies[colour]:
            copy.wait()
    step = CAP // (len(outs) - 1)
    for i, got in enumerate((got1, got0)):
        halves = ((made[i * CAP : (i + 1) * CAP, :], core), (got[...], 1 - core))
        for column in range(ZH):
            k = (zh - column + ZH) % ZH
            total = 0.0
            for colour in range(2):
                part = ((zh + colour) % 2) ^ table[2]
                for hidden, side in halves:
                    w = held[k % 2, k // 2, part, pl.ds(side * HALF, HALF)]
                    total = total + dot(
                        hidden[:, colour * COLS : (colour + 1) * COLS],
                        w.reshape(HALF * ROWS_OUT, COLS),
                    )
            total = total.astype(BF16)
            at = slice(column * COLS, (column + 1) * COLS)
            if i == 1:
                outs[-1][:, at] = total
            else:
                for part, out in enumerate(outs[:-1]):
                    out[:, at] = total[part * step : (part + 1) * step]


def outcome_call(table, made, got, pieces, parts):
    vmem, anywhere = pl.BlockSpec(memory_space=pltpu.VMEM), pl.BlockSpec(memory_space=pl.ANY)
    return pl.pallas_call(
        outcome_kernel,
        in_specs=[pl.BlockSpec(memory_space=pltpu.SMEM)] + [vmem] * 3 + [anywhere] * 8,
        out_specs=[vmem] * (parts + 1),
        out_shape=[jax.ShapeDtypeStruct((CAP // parts, D // 2), BF16)] * parts
        + [jax.ShapeDtypeStruct((CAP, D // 2), BF16)],
        scratch_shapes=[
            pltpu.VMEM((2, 2, ZL, PIECES, ROWS_OUT, COLS), BF16),
            pltpu.SemaphoreType.DMA((2, PIECES)),
        ],
        compiler_params=params(20),
        cost_estimate=SMALL,
        name="outcome",
    )(table, made, *got, *pieces)


def put_kernel(before, table, put, gains, same, *refs):
    cross, out, scale = [ref[...] for ref in refs[before:-2]], refs[-2], refs[-1]
    core = table[1]

    @pl.when(pl.program_id(0) == 0)
    def _():
        scale[...] = column_of(gains[...])

    for values, side in (
        (same[...], core),
        (cross[0] if len(cross) == 1 else jnp.concatenate(cross), 1 - core),
    ):
        at = pl.ds(pl.multiple_of(side * COLS, COLS), COLS)
        rows = (dot(put[...], values) * scale[...]).astype(BF16)
        out[:, at] = rows + refs[0][:, at] if before else rows


def put_call(table, put, gains, same, cross, *before):
    rows = put.shape[0]
    part = pl.BlockSpec((CAP // len(cross), COLS), lambda i, s: (0, i))
    block = pl.BlockSpec((rows, 2 * COLS), lambda i, s: (0, i))
    return pl.pallas_call(
        functools.partial(put_kernel, len(before)),
        grid_spec=pltpu.PrefetchScalarGridSpec(
            num_scalar_prefetch=1,
            grid=(ZH,),
            in_specs=[
                pl.BlockSpec((rows, CAP), lambda i, s: (0, 0)),
                pl.BlockSpec((1, rows), lambda i, s: (0, 0)),
                pl.BlockSpec((CAP, COLS), lambda i, s: (0, i)),
            ]
            + [block] * len(before)
            + [part] * len(cross),
            out_specs=block,
            scratch_shapes=[pltpu.VMEM((rows, 1), F32)],
        ),
        out_shape=jax.ShapeDtypeStruct((rows, D), BF16),
        compiler_params=params(16),
        cost_estimate=LARGE if before else SMALL,
        name="put",
    )(table, put, gains, same, *before, *cross)


def body(
    base_in, base_out, local_in, local_out, mom_in, mom_out, exp_in, exp_out, tokens, routes, gains
):
    zh, core, zl = lax.axis_index("zh"), lax.axis_index("core"), lax.axis_index("zl")
    y, x = lax.axis_index("y"), lax.axis_index("x")
    place = jnp.stack([zh, core, zl, zl]).astype(jnp.int32)
    spots = jnp.asarray(piece_table().reshape(CORE * Y * X, 2 * PIECES))
    spots = lax.dynamic_index_in_dim(spots, (core * Y + y) * X + x, 0, keepdims=False)
    table = jnp.concatenate([place, spots])

    given, kept, b_in, b_out, m_in, m_out = give_call(
        place, (base_in, local_in, exp_in, base_out, local_out, exp_out), (mom_in, mom_out)
    )
    own, *sent = pair_call(kept, lax.ppermute(given, "core", shift(CORE, 1)))
    received = [lax.ppermute(sent[s - 1], "zh", shift(ZH, s)) for s in range(1, ZH)]
    new_base_in, new_base_out, new_mom_in, new_mom_out, kept, given = step_call(
        place, own, received, b_in, m_in, exp_in, b_out, m_out, exp_out
    )

    routes, _ = lax.optimization_barrier((routes, own))
    route = routes[:, 0]
    rank_of = []
    for named in (zl, 1 - zl):
        chosen = route == named
        rank = jnp.cumsum(chosen.astype(jnp.int32)) - 1
        rank_of.append(jnp.where(chosen, rank, -1))
    slots = jnp.arange(CAP, dtype=jnp.int32)
    pick_own, pick_got = [(slots[:, None] == r[None, :]).astype(BF16) for r in rank_of]
    put_own, put_got = [(r[:, None] == slots[None, :]).astype(BF16) for r in rank_of]
    tokens_own = dot(pick_own, tokens).astype(BF16)
    tokens_sent = dot(pick_got, tokens).astype(BF16)
    other_own = lax.ppermute(tokens_own, "core", shift(CORE, 1))

    taken = lax.ppermute(given, "zl", shift(ZL, 1))
    kept, taken, tokens_sent, other_own = lax.optimization_barrier(
        (kept, taken, tokens_sent, other_own)
    )
    both = jnp.stack([kept, taken])
    column = [both] + [lax.ppermute(both, "zh", shift(ZH, s)) for s in range(1, ZH)]
    *column, tokens_sent = lax.optimization_barrier((*column, tokens_sent))

    tokens_got = lax.ppermute(tokens_sent, COLUMN, column_pairs(1, 0))
    held = [jnp.stack([column[c], column[c + 2]])[None] for c in (0, 1)]

    def exchange(arrays, axes, turn):
        return [
            lax.ppermute(a, ("core", axis), flip_pairs(turn)) for a, axis in zip(arrays, axes)
        ]

    for turn in range(2):
        held = [jnp.concatenate(pair) for pair in zip(held, exchange(held, ("x", "y"), turn))]
    first = exchange(held, ("y", "x"), 0)
    second = exchange(held, ("y", "x"), 1)
    third = exchange(first, ("y", "x"), 1)
    pieces = [part[c] for c in range(2) for part in (held, first, second, third)]
    other_got = lax.ppermute(tokens_got, "core", shift(CORE, 1))

    def swap(arrays):
        return [lax.ppermute(a, "core", shift(CORE, 1)) for a in arrays]

    far = hidden_call(table, (other_got, tokens_got), pieces, 1)
    far_got = swap(far[1:])
    other_own, tokens_own, _ = lax.optimization_barrier((other_own, tokens_own, far[0]))
    near = hidden_call(table, (other_own, tokens_own), pieces, 1)
    near_got = swap(near[1:])
    far_other, far_mine = outcome_call(table, far[0], far_got, pieces, 1)
    far_other, far_mine, near, near_got = lax.optimization_barrier(
        (far_other, far_mine, near[0], near_got)
    )
    back_same = lax.ppermute(far_mine, COLUMN, column_pairs(-1, 0))
    back_cross = lax.ppermute(far_other, COLUMN, column_pairs(-1, 1))
    *near_other, near_mine = outcome_call(table, near, near_got, pieces, 4)
    near_cross = swap(near_other)
    line = gains[None, :]
    mixed = put_call(table, put_own, line, near_mine, near_cross)
    mixed = put_call(table, put_got, line, back_same, [back_cross], mixed)
    return (new_base_in, new_base_out, new_mom_in, new_mom_out, mixed)


def solution(mesh):
    split = Mesh(mesh.devices.reshape(ZH, CORE, ZL, Y, X), AXES)
    in_specs = (
        P(None, FSDP, None),
        P(None, FSDP, None),
        P(ISLAND, None, FSDP, None),
        P(ISLAND, None, FSDP, None),
        P(None, FSDP, None),
        P(None, FSDP, None),
        P(None, FSDP),
        P(None, FSDP),
        P(ISLAND + FSDP, None),
        P(ISLAND + FSDP, None),
        P(ISLAND + FSDP),
    )
    out_specs = (
        P(None, FSDP, ISLAND),
        P(None, FSDP, ISLAND),
        P(None, FSDP, ISLAND),
        P(None, FSDP, ISLAND),
        P(ISLAND + FSDP, None),
    )
    return jax.shard_map(body, mesh=split, in_specs=in_specs, out_specs=out_specs, check_vma=False)
```

```python
import functools

import jax
import jax.numpy as jnp
import numpy as np
from jax import lax
from jax.experimental import pallas as pl
from jax.experimental.pallas import tpu as pltpu
from jax.sharding import Mesh
from jax.sharding import PartitionSpec as P

D = 2048
FF = 1024
CAP = 320
ZH, CORE, ZL, Y, X = 4, 2, 2, 4, 4
AXES = ("zh", "core", "zl", "y", "x")
ISLAND = ("zh", "core")
FSDP = ("zl", "y", "x")
COLUMN = ("zh", "core", "zl")
GROUPS = ZH * CORE
COLS = 256
ROWS_IN, ROWS_OUT = 64, 32
ROWS = ROWS_IN + ROWS_OUT
PIECES = Y * X
HALF = PIECES // 2
SETS = 2
BF16, F32 = jnp.bfloat16, jnp.float32

MASKS = ((1, 3), (3, 1))
REACH = tuple((0, a, b, a ^ b) for a, b in MASKS)


def piece_table():
    table = np.zeros((CORE, Y, X, 2, PIECES), np.int32)
    for core in range(CORE):
        for y in range(Y):
            for x in range(X):
                for p in range(PIECES):
                    first, second = REACH[core][p % 4], REACH[core][p // 4]
                    table[core, y, x, 0, p] = (y ^ second) * X + (x ^ first)
                    table[core, y, x, 1, p] = (y ^ first) * X + (x ^ second)
    return table


def shift(size, step):
    return [(i, (i + step) % size) for i in range(size)]


def flip_pairs(turn):
    return [
        (core * 4 + i, core * 4 + (i ^ MASKS[core][turn])) for core in range(CORE) for i in range(4)
    ]


def column_pairs(sign, swap):
    pairs = []
    for zh in range(ZH):
        for core in range(CORE):
            for zl in range(ZL):
                z = (zh * ZL + zl + sign * (1 - 2 * core)) % (ZH * ZL)
                sender = core ^ swap
                pairs.append(
                    ((zh * CORE + sender) * ZL + zl, ((z // ZL) * CORE + core) * ZL + z % ZL)
                )
    return pairs


def dot(a, b):
    return jnp.dot(a, b, preferred_element_type=F32)


def params(mib=48):
    return pltpu.CompilerParams(vmem_limit_bytes=mib * 2**20)


def column_of(line):
    size = line.shape[1]
    eye = lax.broadcasted_iota(jnp.int32, (size, size), 0) == lax.broadcasted_iota(
        jnp.int32, (size, size), 1
    )
    return jnp.sum(jnp.where(eye, line, 0.0), axis=1, keepdims=True)


def row_exponents(expo):
    return jnp.stack([column_of(expo[e : e + 1, :].astype(F32)) for e in range(2)])


def give_kernel(
    place, b_in, l_in, e_in, b_out, l_out, e_out, m_in, m_out,
    given, kept, ob_in, ob_out, om_in, om_out, sems,
):
    zh, core = place[0], place[1]
    mine = pl.ds(pl.multiple_of((zh * CORE + core) * COLS, COLS), COLS)
    copies = [
        pltpu.make_async_copy(whole.at[:, :, mine], out, sems.at[i])
        for i, (whole, out) in enumerate(((m_in, om_in), (m_out, om_out)))
    ]
    for copy in copies:
        copy.start()
    ob_in[...] = b_in[:, :, mine]
    ob_out[...] = b_out[:, :, mine]
    for base, local, expo, rows, first in (
        (b_in, l_in, e_in, ROWS_IN, 0),
        (b_out, l_out, e_out, ROWS_OUT, ROWS_IN),
    ):
        scale = jnp.exp2(-row_exponents(expo))
        for step in range(ZH):
            for out, side in ((given, 1 - core), (kept, core)):
                column = (((zh + step) % ZH) * CORE + side) * COLS
                at = pl.ds(pl.multiple_of(column, COLS), COLS)
                quant = (base[:, :, at] - local[0, :, :, at].astype(F32)) * scale
                out[step, :, first : first + rows] = jnp.clip(quant, -127.0, 127.0).astype(BF16)
    for copy in copies:
        copy.wait()


def give_call(place, arrays, moments):
    vmem, anywhere = pl.BlockSpec(memory_space=pltpu.VMEM), pl.BlockSpec(memory_space=pl.ANY)
    own = [jax.ShapeDtypeStruct((2, r, COLS), F32) for r in (ROWS_IN, ROWS_OUT) * 2]
    return pl.pallas_call(
        give_kernel,
        in_specs=[pl.BlockSpec(memory_space=pltpu.SMEM)] + [vmem] * 6 + [anywhere] * 2,
        out_specs=[vmem] * 6,
        out_shape=[jax.ShapeDtypeStruct((ZH, 2, ROWS, COLS), BF16)] * 2 + own,
        scratch_shapes=[pltpu.SemaphoreType.DMA((2,))],
        compiler_params=params(60),
        cost_estimate=pl.CostEstimate(flops=10**6, bytes_accessed=4 * 2**20, transcendentals=0),
        name="give",
    )(place, *arrays, *moments)


def pair_kernel(kept, taken, own, *sent):
    for step, out in enumerate((own,) + sent):
        out[...] = (kept[step].astype(F32) + taken[step].astype(F32)).astype(out.dtype)


def pair_call(kept, taken):
    vmem = pl.BlockSpec(memory_space=pltpu.VMEM)
    return pl.pallas_call(
        pair_kernel,
        in_specs=[vmem] * 2,
        out_specs=[vmem] * ZH,
        out_shape=[jax.ShapeDtypeStruct((2, ROWS, COLS), F32)]
        + [jax.ShapeDtypeStruct((2, ROWS, COLS), BF16)] * (ZH - 1),
        compiler_params=params(16),
        cost_estimate=pl.CostEstimate(flops=10**6, bytes_accessed=2 * 2**20, transcendentals=0),
        name="pair",
    )(kept, taken)


def step_kernel(
    place, own, r1, r2, r3, b_in, m_in, e_in, b_out, m_out, e_out,
    nb_in, nb_out, nm_in, nm_out, kept, given, weights,
):
    total = own[...] + r1[...].astype(F32) + r2[...].astype(F32) + r3[...].astype(F32)

    def nesterov(base, moment, part, expo):
        grad = part * jnp.exp2(expo) / GROUPS
        new_mom = 0.9 * moment + grad
        return base - 0.7 * (grad + 0.9 * new_mom), new_mom

    nb_in[...], nm_in[...] = nesterov(
        b_in[...], m_in[...], total[:, :ROWS_IN], row_exponents(e_in)
    )
    nb_out[...], nm_out[...] = nesterov(
        b_out[...], m_out[...], total[:, ROWS_IN:], row_exponents(e_out)
    )
    weights[:, :ROWS_IN] = nb_in[...].astype(BF16)
    weights[:, ROWS_IN:] = nb_out[...].astype(BF16)
    kept[...] = weights[place[2]]
    given[...] = weights[1 - place[2]]


def step_call(place, own, received, base_in, mom_in, exp_in, base_out, mom_out, exp_out):
    vmem = pl.BlockSpec(memory_space=pltpu.VMEM)
    new = [(2, r, COLS) for r in (ROWS_IN, ROWS_OUT, ROWS_IN, ROWS_OUT)]
    return pl.pallas_call(
        step_kernel,
        in_specs=[pl.BlockSpec(memory_space=pltpu.SMEM)] + [vmem] * 10,
        out_specs=[vmem] * 6,
        out_shape=[jax.ShapeDtypeStruct(shape, F32) for shape in new]
        + [jax.ShapeDtypeStruct((ROWS, COLS), BF16)] * 2,
        scratch_shapes=[pltpu.VMEM((2, ROWS, COLS), BF16)],
        compiler_params=params(16),
        cost_estimate=pl.CostEstimate(flops=10**6, bytes_accessed=2 * 2**20, transcendentals=0),
        name="step",
    )(place, own, *received, base_in, mom_in, exp_in, base_out, mom_out, exp_out)


def load_pieces(table, pieces, held, sems, colour, rows):
    copies = []
    for p in range(PIECES):
        copies.append(
            pltpu.make_async_copy(
                pieces[colour * 4 + p // 4].at[p % 4, :, :, rows],
                held.at[colour, :, :, table[4 + colour * PIECES + p]],
                sems.at[colour, p],
            )
        )
    for copy in copies:
        copy.start()
    return copies


def hidden_kernel(parts, table, *refs):
    sets, pieces, outs, (x, held, x_sems, sems) = (
        refs[:SETS],
        refs[SETS : SETS + 8],
        refs[SETS + 8 : -4],
        refs[-4:],
    )
    zh, zl = table[0], table[2]
    rows = pl.ds(0, ROWS_IN)
    loads = [pltpu.make_async_copy(sets[i], x.at[i], x_sems.at[i]) for i in range(SETS)]
    loads[0].start()
    copies = [load_pieces(table, pieces, held, sems, 0, rows)]
    loads[1].start()
    copies.append(load_pieces(table, pieces, held, sems, 1, rows))
    gates = (zh // 2, jnp.where((zh == 0) | (zh == 3), 1, 0))
    for colour in range(2):
        for copy in copies[colour]:
            copy.wait()
        for i in range(SETS):
            if colour == 0:
                loads[i].wait()

            def product(k):
                return sum(
                    dot(
                        x[i, :, part * 1024 : (part + 1) * 1024],
                        held[colour, k, part ^ zl].reshape(PIECES * ROWS_IN, COLS),
                    )
                    for part in range(ZL)
                )

            gate, up = product(gates[colour]), product(1 - gates[colour])
            value = (jax.nn.silu(gate) * up).astype(BF16)
            at = slice(colour * COLS, (colour + 1) * COLS)
            outs[0][i * CAP : (i + 1) * CAP, at] = value
            for part in range(parts):
                step = CAP // parts
                outs[1 + i * parts + part][:, at] = value[part * step : (part + 1) * step]


SMALL = pl.CostEstimate(flops=10**3, bytes_accessed=10**3, transcendentals=0)
LARGE = pl.CostEstimate(flops=10**9, bytes_accessed=6 * 2**20, transcendentals=0)


def hidden_call(table, sets, pieces, parts):
    vmem, anywhere = pl.BlockSpec(memory_space=pltpu.VMEM), pl.BlockSpec(memory_space=pl.ANY)
    return pl.pallas_call(
        functools.partial(hidden_kernel, parts),
        in_specs=[pl.BlockSpec(memory_space=pltpu.SMEM)] + [anywhere] * (SETS + 8),
        out_specs=[vmem] * (1 + SETS * parts),
        out_shape=[jax.ShapeDtypeStruct((SETS * CAP, FF // 2), BF16)]
        + [jax.ShapeDtypeStruct((CAP // parts, FF // 2), BF16)] * (SETS * parts),
        scratch_shapes=[
            pltpu.VMEM((SETS, CAP, D), BF16),
            pltpu.VMEM((2, 2, ZL, PIECES, ROWS_IN, COLS), BF16),
            pltpu.SemaphoreType.DMA((SETS,)),
            pltpu.SemaphoreType.DMA((2, PIECES)),
        ],
        compiler_params=params(24),
        cost_estimate=SMALL,
        name="hidden",
    )(table, *sets, *pieces)


def outcome_kernel(table, made, got0, got1, *refs):
    pieces, outs, (held, sems) = refs[:8], refs[8:-2], refs[-2:]
    zh, core = table[0], table[1]
    rows = pl.ds(ROWS_IN, ROWS_OUT)
    copies = [load_pieces(table, pieces, held, sems, colour, rows) for colour in range(2)]
    for colour in range(2):
        for copy in copies[colour]:
            copy.wait()
    step = CAP // (len(outs) - 1)
    for i, got in enumerate((got1, got0)):
        halves = ((made[i * CAP : (i + 1) * CAP, :], core), (got[...], 1 - core))
        for column in range(ZH):
            k = (zh - column + ZH) % ZH
            total = 0.0
            for colour in range(2):
                part = ((zh + colour) % 2) ^ table[2]
                for hidden, side in halves:
                    w = held[k % 2, k // 2, part, pl.ds(side * HALF, HALF)]
                    total = total + dot(
                        hidden[:, colour * COLS : (colour + 1) * COLS],
                        w.reshape(HALF * ROWS_OUT, COLS),
                    )
            total = total.astype(BF16)
            at = slice(column * COLS, (column + 1) * COLS)
            if i == 1:
                outs[-1][:, at] = total
            else:
                for part, out in enumerate(outs[:-1]):
                    out[:, at] = total[part * step : (part + 1) * step]


def outcome_call(table, made, got, pieces, parts):
    vmem, anywhere = pl.BlockSpec(memory_space=pltpu.VMEM), pl.BlockSpec(memory_space=pl.ANY)
    return pl.pallas_call(
        outcome_kernel,
        in_specs=[pl.BlockSpec(memory_space=pltpu.SMEM)] + [vmem] * 3 + [anywhere] * 8,
        out_specs=[vmem] * (parts + 1),
        out_shape=[jax.ShapeDtypeStruct((CAP // parts, D // 2), BF16)] * parts
        + [jax.ShapeDtypeStruct((CAP, D // 2), BF16)],
        scratch_shapes=[
            pltpu.VMEM((2, 2, ZL, PIECES, ROWS_OUT, COLS), BF16),
            pltpu.SemaphoreType.DMA((2, PIECES)),
        ],
        compiler_params=params(20),
        cost_estimate=SMALL,
        name="outcome",
    )(table, made, *got, *pieces)


def put_kernel(before, table, put, gains, same, *refs):
    cross, out, scale = [ref[...] for ref in refs[before:-2]], refs[-2], refs[-1]
    core = table[1]

    @pl.when(pl.program_id(0) == 0)
    def _():
        scale[...] = column_of(gains[...])

    for values, side in (
        (same[...], core),
        (cross[0] if len(cross) == 1 else jnp.concatenate(cross), 1 - core),
    ):
        rows = (dot(put[...], values) * scale[...]).astype(BF16)
        for group in range(2):
            at = pl.ds(pl.multiple_of((group * CORE + side) * COLS, COLS), COLS)
            part = rows[:, group * COLS : (group + 1) * COLS]
            out[:, at] = part + refs[0][:, at] if before else part


def put_call(table, put, gains, same, cross, *before):
    rows = put.shape[0]
    part = pl.BlockSpec((CAP // len(cross), 2 * COLS), lambda i, s: (0, i))
    block = pl.BlockSpec((rows, 4 * COLS), lambda i, s: (0, i))
    return pl.pallas_call(
        functools.partial(put_kernel, len(before)),
        grid_spec=pltpu.PrefetchScalarGridSpec(
            num_scalar_prefetch=1,
            grid=(ZH // 2,),
            in_specs=[
                pl.BlockSpec((rows, CAP), lambda i, s: (0, 0)),
                pl.BlockSpec((1, rows), lambda i, s: (0, 0)),
                pl.BlockSpec((CAP, 2 * COLS), lambda i, s: (0, i)),
            ]
            + [block] * len(before)
            + [part] * len(cross),
            out_specs=block,
            scratch_shapes=[pltpu.VMEM((rows, 1), F32)],
        ),
        out_shape=jax.ShapeDtypeStruct((rows, D), BF16),
        compiler_params=params(20),
        cost_estimate=LARGE if before else SMALL,
        name="put",
    )(table, put, gains, same, *before, *cross)


def body(
    base_in, base_out, local_in, local_out, mom_in, mom_out, exp_in, exp_out, tokens, routes, gains
):
    zh, core, zl = lax.axis_index("zh"), lax.axis_index("core"), lax.axis_index("zl")
    y, x = lax.axis_index("y"), lax.axis_index("x")
    place = jnp.stack([zh, core, zl, zl]).astype(jnp.int32)
    spots = jnp.asarray(piece_table().reshape(CORE * Y * X, 2 * PIECES))
    spots = lax.dynamic_index_in_dim(spots, (core * Y + y) * X + x, 0, keepdims=False)
    table = jnp.concatenate([place, spots])

    given, kept, b_in, b_out, m_in, m_out = give_call(
        place, (base_in, local_in, exp_in, base_out, local_out, exp_out), (mom_in, mom_out)
    )
    own, *sent = pair_call(kept, lax.ppermute(given, "core", shift(CORE, 1)))
    received = [lax.ppermute(sent[s - 1], "zh", shift(ZH, s)) for s in range(1, ZH)]
    new_base_in, new_base_out, new_mom_in, new_mom_out, kept, given = step_call(
        place, own, received, b_in, m_in, exp_in, b_out, m_out, exp_out
    )

    routes, _ = lax.optimization_barrier((routes, own))
    route = routes[:, 0]
    rank_of = []
    for named in (zl, 1 - zl):
        chosen = route == named
        rank = jnp.cumsum(chosen.astype(jnp.int32)) - 1
        rank_of.append(jnp.where(chosen, rank, -1))
    slots = jnp.arange(CAP, dtype=jnp.int32)
    pick_own, pick_got = [(slots[:, None] == r[None, :]).astype(BF16) for r in rank_of]
    put_own, put_got = [(r[:, None] == slots[None, :]).astype(BF16) for r in rank_of]
    tokens_own = dot(pick_own, tokens).astype(BF16)
    tokens_sent = dot(pick_got, tokens).astype(BF16)
    tokens_own, given = lax.optimization_barrier((tokens_own, given))
    other_own = lax.ppermute(tokens_own, "core", shift(CORE, 1))

    taken = lax.ppermute(given, "zl", shift(ZL, 1))
    kept, taken, tokens_sent, other_own = lax.optimization_barrier(
        (kept, taken, tokens_sent, other_own)
    )
    both = jnp.stack([kept, taken])
    column = [both] + [lax.ppermute(both, "zh", shift(ZH, s)) for s in range(1, ZH)]
    *column, tokens_sent = lax.optimization_barrier((*column, tokens_sent))

    tokens_got = lax.ppermute(tokens_sent, COLUMN, column_pairs(1, 0))
    held = [jnp.stack([column[c], column[c + 2]])[None] for c in (0, 1)]

    def exchange(arrays, axes, turn):
        return [
            lax.ppermute(a, ("core", axis), flip_pairs(turn)) for a, axis in zip(arrays, axes)
        ]

    for turn in range(2):
        held = [jnp.concatenate(pair) for pair in zip(held, exchange(held, ("x", "y"), turn))]
    first = exchange(held, ("y", "x"), 0)
    second = exchange(held, ("y", "x"), 1)
    third = exchange(first, ("y", "x"), 1)
    pieces = [part[c] for c in range(2) for part in (held, first, second, third)]
    other_got = lax.ppermute(tokens_got, "core", shift(CORE, 1))

    def swap(arrays):
        return [lax.ppermute(a, "core", shift(CORE, 1)) for a in arrays]

    far = hidden_call(table, (other_got, tokens_got), pieces, 1)
    far_got = swap(far[1:])
    other_own, tokens_own, _ = lax.optimization_barrier((other_own, tokens_own, far[0]))
    near = hidden_call(table, (other_own, tokens_own), pieces, 1)
    near_got = swap(near[1:])
    far_other, far_mine = outcome_call(table, far[0], far_got, pieces, 1)
    far_other, far_mine, near, near_got = lax.optimization_barrier(
        (far_other, far_mine, near[0], near_got)
    )
    back_same = lax.ppermute(far_mine, COLUMN, column_pairs(-1, 0))
    back_cross = lax.ppermute(far_other, COLUMN, column_pairs(-1, 1))
    *near_other, near_mine = outcome_call(table, near, near_got, pieces, 4)
    near_cross = swap(near_other)
    line = gains[None, :]
    mixed = put_call(table, put_own, line, near_mine, near_cross)
    mixed = put_call(table, put_got, line, back_same, [back_cross], mixed)
    return (new_base_in, new_base_out, new_mom_in, new_mom_out, mixed)


def solution(mesh):
    split = Mesh(mesh.devices.reshape(ZH, CORE, ZL, Y, X), AXES)
    in_specs = (
        P(None, FSDP, None),
        P(None, FSDP, None),
        P(ISLAND, None, FSDP, None),
        P(ISLAND, None, FSDP, None),
        P(None, FSDP, None),
        P(None, FSDP, None),
        P(None, FSDP),
        P(None, FSDP),
        P(ISLAND + FSDP, None),
        P(ISLAND + FSDP, None),
        P(ISLAND + FSDP),
    )
    out_specs = (
        P(None, FSDP, ISLAND),
        P(None, FSDP, ISLAND),
        P(None, FSDP, ISLAND),
        P(None, FSDP, ISLAND),
        P(ISLAND + FSDP, None),
    )
    return jax.shard_map(body, mesh=split, in_specs=in_specs, out_specs=out_specs, check_vma=False)
```

```python
import functools

import jax
import jax.numpy as jnp
import numpy as np
from jax import lax
from jax.experimental import pallas as pl
from jax.experimental.pallas import tpu as pltpu
from jax.sharding import Mesh
from jax.sharding import PartitionSpec as P

D = 2048
FF = 1024
CAP = 320
ZH, CORE, ZL, Y, X = 4, 2, 2, 4, 4
AXES = ("zh", "core", "zl", "y", "x")
ISLAND = ("zh", "core")
FSDP = ("zl", "y", "x")
COLUMN = ("zh", "core", "zl")
GROUPS = ZH * CORE
FAR_FIRST = (2, 1, 3)
COLS = 256
ROWS_IN, ROWS_OUT = 64, 32
ROWS = ROWS_IN + ROWS_OUT
PIECES = Y * X
HALF = PIECES // 2
SETS = 2
BF16, F32 = jnp.bfloat16, jnp.float32

MASKS = ((1, 3), (3, 1))
REACH = tuple((0, a, b, a ^ b) for a, b in MASKS)


def piece_table():
    table = np.zeros((CORE, Y, X, 2, PIECES), np.int32)
    for core in range(CORE):
        for y in range(Y):
            for x in range(X):
                for p in range(PIECES):
                    first, second = REACH[core][p % 4], REACH[core][p // 4]
                    table[core, y, x, 0, p] = (y ^ second) * X + (x ^ first)
                    table[core, y, x, 1, p] = (y ^ first) * X + (x ^ second)
    return table


def shift(size, step):
    return [(i, (i + step) % size) for i in range(size)]


def flip_pairs(turn):
    return [
        (core * 4 + i, core * 4 + (i ^ MASKS[core][turn])) for core in range(CORE) for i in range(4)
    ]


def column_pairs(sign, swap):
    pairs = []
    for zh in range(ZH):
        for core in range(CORE):
            for zl in range(ZL):
                z = (zh * ZL + zl + sign * (1 - 2 * core)) % (ZH * ZL)
                sender = core ^ swap
                pairs.append(
                    ((zh * CORE + sender) * ZL + zl, ((z // ZL) * CORE + core) * ZL + z % ZL)
                )
    return pairs


def dot(a, b):
    return jnp.dot(a, b, preferred_element_type=F32)


def params(mib=48):
    return pltpu.CompilerParams(vmem_limit_bytes=mib * 2**20)


def column_of(line):
    size = line.shape[1]
    eye = lax.broadcasted_iota(jnp.int32, (size, size), 0) == lax.broadcasted_iota(
        jnp.int32, (size, size), 1
    )
    return jnp.sum(jnp.where(eye, line, 0.0), axis=1, keepdims=True)


def row_exponents(expo):
    return jnp.stack([column_of(expo[e : e + 1, :].astype(F32)) for e in range(2)])


def give_kernel(
    place, b_in, l_in, e_in, b_out, l_out, e_out, m_in, m_out,
    given, kept, ob_in, ob_out, om_in, om_out, sems,
):
    zh, core = place[0], place[1]
    mine = pl.ds(pl.multiple_of((zh * CORE + core) * COLS, COLS), COLS)
    copies = [
        pltpu.make_async_copy(whole.at[:, :, mine], out, sems.at[i])
        for i, (whole, out) in enumerate(((m_in, om_in), (m_out, om_out)))
    ]
    for copy in copies:
        copy.start()
    ob_in[...] = b_in[:, :, mine]
    ob_out[...] = b_out[:, :, mine]
    for base, local, expo, rows, first in (
        (b_in, l_in, e_in, ROWS_IN, 0),
        (b_out, l_out, e_out, ROWS_OUT, ROWS_IN),
    ):
        scale = jnp.exp2(-row_exponents(expo))
        for step in range(ZH):
            for out, side in ((given, 1 - core), (kept, core)):
                column = (((zh + step) % ZH) * CORE + side) * COLS
                at = pl.ds(pl.multiple_of(column, COLS), COLS)
                quant = (base[:, :, at] - local[0, :, :, at].astype(F32)) * scale
                out[step, :, first : first + rows] = jnp.clip(quant, -127.0, 127.0).astype(BF16)
    for copy in copies:
        copy.wait()


def give_call(place, arrays, moments):
    vmem, anywhere = pl.BlockSpec(memory_space=pltpu.VMEM), pl.BlockSpec(memory_space=pl.ANY)
    own = [jax.ShapeDtypeStruct((2, r, COLS), F32) for r in (ROWS_IN, ROWS_OUT) * 2]
    return pl.pallas_call(
        give_kernel,
        in_specs=[pl.BlockSpec(memory_space=pltpu.SMEM)] + [vmem] * 6 + [anywhere] * 2,
        out_specs=[vmem] * 6,
        out_shape=[jax.ShapeDtypeStruct((ZH, 2, ROWS, COLS), BF16)] * 2 + own,
        scratch_shapes=[pltpu.SemaphoreType.DMA((2,))],
        compiler_params=params(60),
        cost_estimate=pl.CostEstimate(flops=10**6, bytes_accessed=4 * 2**20, transcendentals=0),
        name="give",
    )(place, *arrays, *moments)


def pair_kernel(kept, taken, own, *sent):
    for step, out in enumerate((own,) + sent):
        out[...] = (kept[step].astype(F32) + taken[step].astype(F32)).astype(out.dtype)


def pair_call(kept, taken):
    vmem = pl.BlockSpec(memory_space=pltpu.VMEM)
    return pl.pallas_call(
        pair_kernel,
        in_specs=[vmem] * 2,
        out_specs=[vmem] * ZH,
        out_shape=[jax.ShapeDtypeStruct((2, ROWS, COLS), F32)]
        + [jax.ShapeDtypeStruct((2, ROWS, COLS), BF16)] * (ZH - 1),
        compiler_params=params(16),
        cost_estimate=pl.CostEstimate(flops=10**6, bytes_accessed=2 * 2**20, transcendentals=0),
        name="pair",
    )(kept, taken)


def step_kernel(
    place, own, r1, r2, r3, b_in, m_in, e_in, b_out, m_out, e_out,
    nb_in, nb_out, nm_in, nm_out, kept, given, weights,
):
    total = own[...] + r1[...].astype(F32) + r2[...].astype(F32) + r3[...].astype(F32)

    def nesterov(base, moment, part, expo):
        grad = part * jnp.exp2(expo) / GROUPS
        new_mom = 0.9 * moment + grad
        return base - 0.7 * (grad + 0.9 * new_mom), new_mom

    nb_in[...], nm_in[...] = nesterov(
        b_in[...], m_in[...], total[:, :ROWS_IN], row_exponents(e_in)
    )
    nb_out[...], nm_out[...] = nesterov(
        b_out[...], m_out[...], total[:, ROWS_IN:], row_exponents(e_out)
    )
    weights[:, :ROWS_IN] = nb_in[...].astype(BF16)
    weights[:, ROWS_IN:] = nb_out[...].astype(BF16)
    kept[...] = weights[place[2]]
    given[...] = weights[1 - place[2]]


def step_call(place, own, received, base_in, mom_in, exp_in, base_out, mom_out, exp_out):
    vmem = pl.BlockSpec(memory_space=pltpu.VMEM)
    new = [(2, r, COLS) for r in (ROWS_IN, ROWS_OUT, ROWS_IN, ROWS_OUT)]
    return pl.pallas_call(
        step_kernel,
        in_specs=[pl.BlockSpec(memory_space=pltpu.SMEM)] + [vmem] * 10,
        out_specs=[vmem] * 6,
        out_shape=[jax.ShapeDtypeStruct(shape, F32) for shape in new]
        + [jax.ShapeDtypeStruct((ROWS, COLS), BF16)] * 2,
        scratch_shapes=[pltpu.VMEM((2, ROWS, COLS), BF16)],
        compiler_params=params(16),
        cost_estimate=pl.CostEstimate(flops=10**6, bytes_accessed=2 * 2**20, transcendentals=0),
        name="step",
    )(place, own, *received, base_in, mom_in, exp_in, base_out, mom_out, exp_out)


def load_pieces(table, pieces, held, sems, colour, rows):
    copies = []
    for p in range(PIECES):
        copies.append(
            pltpu.make_async_copy(
                pieces[colour * 4 + p // 4].at[p % 4, :, :, rows],
                held.at[colour, :, :, table[4 + colour * PIECES + p]],
                sems.at[colour, p],
            )
        )
    for copy in copies:
        copy.start()
    return copies


def hidden_kernel(parts, table, *refs):
    sets, pieces, outs, (x, held, x_sems, sems) = (
        refs[:SETS],
        refs[SETS : SETS + 8],
        refs[SETS + 8 : -4],
        refs[-4:],
    )
    zh, zl = table[0], table[2]
    rows = pl.ds(0, ROWS_IN)
    loads = [pltpu.make_async_copy(sets[i], x.at[i], x_sems.at[i]) for i in range(SETS)]
    loads[0].start()
    copies = [load_pieces(table, pieces, held, sems, 0, rows)]
    loads[1].start()
    copies.append(load_pieces(table, pieces, held, sems, 1, rows))
    gates = (zh // 2, jnp.where((zh == 0) | (zh == 3), 1, 0))
    for colour in range(2):
        for copy in copies[colour]:
            copy.wait()
        for i in range(SETS):
            if colour == 0:
                loads[i].wait()

            def product(k):
                return sum(
                    dot(
                        x[i, :, part * 1024 : (part + 1) * 1024],
                        held[colour, k, part ^ zl].reshape(PIECES * ROWS_IN, COLS),
                    )
                    for part in range(ZL)
                )

            gate, up = product(gates[colour]), product(1 - gates[colour])
            value = (jax.nn.silu(gate) * up).astype(BF16)
            at = slice(colour * COLS, (colour + 1) * COLS)
            outs[0][i * CAP : (i + 1) * CAP, at] = value
            for part in range(parts):
                step = CAP // parts
                outs[1 + i * parts + part][:, at] = value[part * step : (part + 1) * step]


SMALL = pl.CostEstimate(flops=10**3, bytes_accessed=10**3, transcendentals=0)
LARGE = pl.CostEstimate(flops=10**9, bytes_accessed=6 * 2**20, transcendentals=0)


def hidden_call(table, sets, pieces, parts):
    vmem, anywhere = pl.BlockSpec(memory_space=pltpu.VMEM), pl.BlockSpec(memory_space=pl.ANY)
    return pl.pallas_call(
        functools.partial(hidden_kernel, parts),
        in_specs=[pl.BlockSpec(memory_space=pltpu.SMEM)] + [anywhere] * (SETS + 8),
        out_specs=[vmem] * (1 + SETS * parts),
        out_shape=[jax.ShapeDtypeStruct((SETS * CAP, FF // 2), BF16)]
        + [jax.ShapeDtypeStruct((CAP // parts, FF // 2), BF16)] * (SETS * parts),
        scratch_shapes=[
            pltpu.VMEM((SETS, CAP, D), BF16),
            pltpu.VMEM((2, 2, ZL, PIECES, ROWS_IN, COLS), BF16),
            pltpu.SemaphoreType.DMA((SETS,)),
            pltpu.SemaphoreType.DMA((2, PIECES)),
        ],
        compiler_params=params(24),
        cost_estimate=SMALL,
        name="hidden",
    )(table, *sets, *pieces)


def outcome_kernel(table, made, got0, got1, *refs):
    pieces, outs, (held, sems) = refs[:8], refs[8:-2], refs[-2:]
    zh, core = table[0], table[1]
    rows = pl.ds(ROWS_IN, ROWS_OUT)
    copies = [load_pieces(table, pieces, held, sems, colour, rows) for colour in range(2)]
    for colour in range(2):
        for copy in copies[colour]:
            copy.wait()
    step = CAP // (len(outs) - 1)
    for i, got in enumerate((got1, got0)):
        halves = ((made[i * CAP : (i + 1) * CAP, :], core), (got[...], 1 - core))
        for column in range(ZH):
            k = (zh - column + ZH) % ZH
            total = 0.0
            for colour in range(2):
                part = ((zh + colour) % 2) ^ table[2]
                for hidden, side in halves:
                    w = held[k % 2, k // 2, part, pl.ds(side * HALF, HALF)]
                    total = total + dot(
                        hidden[:, colour * COLS : (colour + 1) * COLS],
                        w.reshape(HALF * ROWS_OUT, COLS),
                    )
            total = total.astype(BF16)
            at = slice(column * COLS, (column + 1) * COLS)
            if i == 1:
                outs[-1][:, at] = total
            else:
                for part, out in enumerate(outs[:-1]):
                    out[:, at] = total[part * step : (part + 1) * step]


def outcome_call(table, made, got, pieces, parts):
    vmem, anywhere = pl.BlockSpec(memory_space=pltpu.VMEM), pl.BlockSpec(memory_space=pl.ANY)
    return pl.pallas_call(
        outcome_kernel,
        in_specs=[pl.BlockSpec(memory_space=pltpu.SMEM)] + [vmem] * 3 + [anywhere] * 8,
        out_specs=[vmem] * (parts + 1),
        out_shape=[jax.ShapeDtypeStruct((CAP // parts, D // 2), BF16)] * parts
        + [jax.ShapeDtypeStruct((CAP, D // 2), BF16)],
        scratch_shapes=[
            pltpu.VMEM((2, 2, ZL, PIECES, ROWS_OUT, COLS), BF16),
            pltpu.SemaphoreType.DMA((2, PIECES)),
        ],
        compiler_params=params(20),
        cost_estimate=SMALL,
        name="outcome",
    )(table, made, *got, *pieces)


def put_kernel(before, table, put, gains, same, *refs):
    cross, out, scale = [ref[...] for ref in refs[before:-2]], refs[-2], refs[-1]
    core = table[1]

    @pl.when(pl.program_id(0) == 0)
    def _():
        scale[...] = column_of(gains[...])

    for values, side in (
        (same[...], core),
        (cross[0] if len(cross) == 1 else jnp.concatenate(cross), 1 - core),
    ):
        rows = (dot(put[...], values) * scale[...]).astype(BF16)
        for group in range(2):
            at = pl.ds(pl.multiple_of((group * CORE + side) * COLS, COLS), COLS)
            part = rows[:, group * COLS : (group + 1) * COLS]
            out[:, at] = part + refs[0][:, at] if before else part


def put_call(table, put, gains, same, cross, *before):
    rows = put.shape[0]
    part = pl.BlockSpec((CAP // len(cross), 2 * COLS), lambda i, s: (0, i))
    block = pl.BlockSpec((rows, 4 * COLS), lambda i, s: (0, i))
    return pl.pallas_call(
        functools.partial(put_kernel, len(before)),
        grid_spec=pltpu.PrefetchScalarGridSpec(
            num_scalar_prefetch=1,
            grid=(ZH // 2,),
            in_specs=[
                pl.BlockSpec((rows, CAP), lambda i, s: (0, 0)),
                pl.BlockSpec((1, rows), lambda i, s: (0, 0)),
                pl.BlockSpec((CAP, 2 * COLS), lambda i, s: (0, i)),
            ]
            + [block] * len(before)
            + [part] * len(cross),
            out_specs=block,
            scratch_shapes=[pltpu.VMEM((rows, 1), F32)],
        ),
        out_shape=jax.ShapeDtypeStruct((rows, D), BF16),
        compiler_params=params(20),
        cost_estimate=LARGE if before else SMALL,
        name="put",
    )(table, put, gains, same, *before, *cross)


def body(
    base_in, base_out, local_in, local_out, mom_in, mom_out, exp_in, exp_out, tokens, routes, gains
):
    zh, core, zl = lax.axis_index("zh"), lax.axis_index("core"), lax.axis_index("zl")
    y, x = lax.axis_index("y"), lax.axis_index("x")
    place = jnp.stack([zh, core, zl, zl]).astype(jnp.int32)
    spots = jnp.asarray(piece_table().reshape(CORE * Y * X, 2 * PIECES))
    spots = lax.dynamic_index_in_dim(spots, (core * Y + y) * X + x, 0, keepdims=False)
    table = jnp.concatenate([place, spots])

    given, kept, b_in, b_out, m_in, m_out = give_call(
        place, (base_in, local_in, exp_in, base_out, local_out, exp_out), (mom_in, mom_out)
    )
    own, *sent = pair_call(kept, lax.ppermute(given, "core", shift(CORE, 1)))
    received = [lax.ppermute(sent[s - 1], "zh", shift(ZH, s)) for s in FAR_FIRST]
    new_base_in, new_base_out, new_mom_in, new_mom_out, kept, given = step_call(
        place, own, received, b_in, m_in, exp_in, b_out, m_out, exp_out
    )

    routes, _ = lax.optimization_barrier((routes, own))
    route = routes[:, 0]
    rank_of = []
    for named in (zl, 1 - zl):
        chosen = route == named
        rank = jnp.cumsum(chosen.astype(jnp.int32)) - 1
        rank_of.append(jnp.where(chosen, rank, -1))
    slots = jnp.arange(CAP, dtype=jnp.int32)
    pick_own, pick_got = [(slots[:, None] == r[None, :]).astype(BF16) for r in rank_of]
    put_own, put_got = [(r[:, None] == slots[None, :]).astype(BF16) for r in rank_of]
    tokens_own = dot(pick_own, tokens).astype(BF16)
    tokens_sent = dot(pick_got, tokens).astype(BF16)
    tokens_own, given = lax.optimization_barrier((tokens_own, given))
    other_own = lax.ppermute(tokens_own, "core", shift(CORE, 1))

    taken = lax.ppermute(given, "zl", shift(ZL, 1))
    kept, taken, tokens_sent, other_own = lax.optimization_barrier(
        (kept, taken, tokens_sent, other_own)
    )
    both = jnp.stack([kept, taken])
    by_step = {s: lax.ppermute(both, "zh", shift(ZH, s)) for s in FAR_FIRST}
    column = [both] + [by_step[s] for s in range(1, ZH)]
    *column, tokens_sent = lax.optimization_barrier((*column, tokens_sent))

    tokens_got = lax.ppermute(tokens_sent, COLUMN, column_pairs(1, 0))
    held = [jnp.stack([column[c], column[c + 2]])[None] for c in (0, 1)]

    def exchange(arrays, axes, turn):
        return [
            lax.ppermute(a, ("core", axis), flip_pairs(turn)) for a, axis in zip(arrays, axes)
        ]

    for turn in range(2):
        held = [jnp.concatenate(pair) for pair in zip(held, exchange(held, ("x", "y"), turn))]
    first = exchange(held, ("y", "x"), 0)
    second = exchange(held, ("y", "x"), 1)
    third = exchange(first, ("y", "x"), 1)
    pieces = [part[c] for c in range(2) for part in (held, first, second, third)]
    other_got = lax.ppermute(tokens_got, "core", shift(CORE, 1))

    def swap(arrays):
        return [lax.ppermute(a, "core", shift(CORE, 1)) for a in arrays]

    far = hidden_call(table, (other_got, tokens_got), pieces, 1)
    far_got = swap(far[1:])
    other_own, tokens_own, _ = lax.optimization_barrier((other_own, tokens_own, far[0]))
    near = hidden_call(table, (other_own, tokens_own), pieces, 1)
    near_got = swap(near[1:])
    far_other, far_mine = outcome_call(table, far[0], far_got, pieces, 1)
    far_other, far_mine, near, near_got = lax.optimization_barrier(
        (far_other, far_mine, near[0], near_got)
    )
    back_same = lax.ppermute(far_mine, COLUMN, column_pairs(-1, 0))
    back_cross = lax.ppermute(far_other, COLUMN, column_pairs(-1, 1))
    *near_other, near_mine = outcome_call(table, near, near_got, pieces, 4)
    near_cross = swap(near_other)
    line = gains[None, :]
    mixed = put_call(table, put_own, line, near_mine, near_cross)
    mixed = put_call(table, put_got, line, back_same, [back_cross], mixed)
    return (new_base_in, new_base_out, new_mom_in, new_mom_out, mixed)


def solution(mesh):
    split = Mesh(mesh.devices.reshape(ZH, CORE, ZL, Y, X), AXES)
    in_specs = (
        P(None, FSDP, None),
        P(None, FSDP, None),
        P(ISLAND, None, FSDP, None),
        P(ISLAND, None, FSDP, None),
        P(None, FSDP, None),
        P(None, FSDP, None),
        P(None, FSDP),
        P(None, FSDP),
        P(ISLAND + FSDP, None),
        P(ISLAND + FSDP, None),
        P(ISLAND + FSDP),
    )
    out_specs = (
        P(None, FSDP, ISLAND),
        P(None, FSDP, ISLAND),
        P(None, FSDP, ISLAND),
        P(None, FSDP, ISLAND),
        P(ISLAND + FSDP, None),
    )
    return jax.shard_map(body, mesh=split, in_specs=in_specs, out_specs=out_specs, check_vma=False)
```
